256 devices in a mesh: ctx: 32 (over z_lo, y, core), kv: 8 (over x, z_hi).
Axes of the slice: x: 4, y: 4, z: 8 (z_hi: 2, z_lo: 4; z = z_hi * 4 + z_lo), core: 2. Of those that a mesh axis runs over, the one named last changes fastest.
Arguments:
- queries: bfloat16 [4096, 128, 128], P('ctx', 'kv'), may hold values from -6 to 6
- keys: bfloat16 [4096, 8, 128], P('ctx', 'kv'), may hold values from -6 to 6
- values: bfloat16 [4096, 8, 128], P('ctx', 'kv'), may hold values from -6 to 6
- outputs: bfloat16 [4096, 128, 128], P('ctx', 'kv'), may hold values from -6 to 6
- out_grad: bfloat16 [4096, 128, 128], P('ctx', 'kv'), may hold values from -6 to 6
- logsumexp: float32 [128, 4096], P('kv', 'ctx'), may hold values from 2 to 5
- doc_lengths: int32 [12], replicated, may hold values from 1 to 512, 4096 in all
- block_order: int32 [32], replicated, may hold values from 0 to 31, each once
Outputs:
- grad_queries: bfloat16 [4096, 128, 128], P('ctx', 'kv')
- grad_keys: bfloat16 [4096, 1024], P(('ctx', 'kv'))
- grad_values: bfloat16 [4096, 1024], P(('ctx', 'kv'))
The draws below stay inside these ranges and needn't reach their ends.
Inputs may be any that keep to these rules, and one draw needn't show every extreme that they name: `doc_lengths`: the documents lie one after another and fill the 4096 tokens; the longest has exactly 512 tokens. A permutation of the 32 blocks: arranged rows i * 128 to i * 128 + 127 hold sequence positions block_order[i] * 128 onward.
All inputs are finite; a program needn't handle non-finite values.
Results may differ from the reference program's by a relative error of at most 0.0051.
Values may be sent and summed in bfloat16 or wider, within the bound.
No kernel may reach another device: no remote copies, remote signals or barrier semaphores. Data moves between devices by JAX's collectives and lax.ppermute only.
A program may use at most 64 MiB of HBM per device.

```python
import math
import jax
import jax.numpy as jnp
import numpy as np
from jax import lax

HG = 16
DH = 128
BLK = 128
NDOC = 12
KVH = 8
H = 128
S = 4096
NB = 32
MOST = 512


def steps_of(own_key, dims, pieces, low, high):
    gain, own = 1.0, jax.random.fold_in(own_key, 6)
    for axis_at, parts in pieces:
        steps = jnp.exp(jax.random.uniform(jax.random.fold_in(own, axis_at), (parts,), jnp.float32, low / len(pieces), high / len(pieces)))
        gain = gain * jnp.repeat(steps, dims[axis_at] // parts).reshape([-1 if axis == axis_at else 1 for axis in range(len(dims))])
    return gain


def split_up(amount, total, reach, lean):
    weights = [(1 << 20) // math.isqrt(standing ** lean) + 1 for standing in range(2, amount + 1)]
    surplus, given = total - reach - (amount - 1), [1] * (amount - 1)
    while surplus > 0:
        movable = [i for i in range(amount - 1) if given[i] < reach]
        mass, left = sum([weights[i] for i in movable]), surplus
        for i in movable:
            extra = min(reach - given[i], max(1, left * weights[i] // mass), surplus)
            given[i] = given[i] + extra
            surplus = surplus - extra
    return np.array([reach] + given)


def ragged(stream_key, count, total, bound, skew):
    if count == 2:
        one = jax.random.randint(stream_key, (), max(1, total - bound), min(bound, total - 1) + 1)
        return jnp.stack([one, total - one])
    lengths = jnp.asarray(split_up(count, total, bound, skew), jnp.int32)
    twos = (count - 1) // 2
    giver, sink = lengths[1:1 + 2 * twos:2], lengths[2:2 + 2 * twos:2]
    margin = jnp.minimum(giver - 1, bound - sink)
    moved = jax.random.randint(jax.random.fold_in(stream_key, 1), (twos,), 0, 1 << 20) % (margin + 1)
    lengths = lengths.at[1:1 + 2 * twos:2].set(giver - moved).at[2:2 + 2 * twos:2].set(sink + moved)
    return lengths[jax.random.permutation(jax.random.fold_in(stream_key, 2), count)]


def noise(rng, dims, width, bound, shards=(), kind=jnp.bfloat16):
    values = width * jax.random.normal(rng, dims, jnp.float32)
    if shards:
        values = values * steps_of(rng, dims, shards, -0.22, 0.18)
    return jnp.clip(values, -bound, bound).astype(kind)


def setup_inputs(seed: int = 0) -> dict:
    arg_keys = jax.random.split(jax.random.key(seed), 9)
    return {
        "queries": noise(arg_keys[0], (S, H, DH), 1.0, 6.0, ((0, 32), (1, 8))),
        "keys": noise(arg_keys[1], (S, KVH, DH), 1.0, 6.0, ((0, 32), (1, 8))),
        "values": noise(arg_keys[2], (S, KVH, DH), 1.0, 6.0, ((0, 32), (1, 8))),
        "outputs": noise(arg_keys[3], (S, H, DH), 0.5, 6.0, ((0, 32), (1, 8))),
        "out_grad": noise(arg_keys[4], (S, H, DH), 1.0, 6.0, ((0, 32), (1, 8))),
        "logsumexp": jnp.clip(2.0 + 3.0 * jax.random.uniform(arg_keys[5], (H, S), jnp.float32) ** steps_of(arg_keys[5], (H, S), ((0, 8), (1, 32)), -0.2, 0.2), 2.0, 5.0),
        "doc_lengths": ragged(arg_keys[6], NDOC, S, MOST, 1).astype(jnp.int32),
        "block_order": jax.random.permutation(arg_keys[7], NB).astype(jnp.int32),
    }


def doc_index(positions, doc_lengths):
    ends = jnp.cumsum(doc_lengths).astype(jnp.int32)
    return jnp.sum((ends[None, :] <= positions[:, None]).astype(jnp.int32), axis=1)


def reference(queries, keys, values, outputs, out_grad, logsumexp, doc_lengths, block_order):
    scale = DH ** -0.5
    rows = jnp.arange(S, dtype=jnp.int32)
    position = (block_order[rows // BLK] * BLK + rows % BLK).astype(jnp.int32)
    query_doc = doc_index(position, doc_lengths)
    key_doc = doc_index(rows, doc_lengths)
    delta = jnp.sum(out_grad.astype(jnp.float32) * outputs.astype(jnp.float32), axis=-1)
    delta = delta.reshape(S, KVH, HG)
    lse_rows = jnp.transpose(logsumexp).reshape(S, KVH, HG)
    grouped_q = queries.reshape(S, KVH, HG, DH)
    grouped_do = out_grad.reshape(S, KVH, HG, DH)
    window = min(MOST + BLK, S)

    def step(carry, block):
        key_total, value_total = carry
        row0 = (block * BLK).astype(jnp.int32)
        q_first = (block_order[block] * BLK).astype(jnp.int32)
        win0 = jnp.clip(q_first + BLK - window, 0, S - window).astype(jnp.int32)
        q_tile = lax.dynamic_slice_in_dim(grouped_q, row0, BLK).astype(jnp.float32)
        do_tile = lax.dynamic_slice_in_dim(grouped_do, row0, BLK).astype(jnp.float32)
        lse_tile = lax.dynamic_slice_in_dim(lse_rows, row0, BLK)
        delta_tile = lax.dynamic_slice_in_dim(delta, row0, BLK)
        key_win = lax.dynamic_slice_in_dim(keys, win0, window).astype(jnp.float32)
        value_win = lax.dynamic_slice_in_dim(values, win0, window).astype(jnp.float32)
        key_pos = win0 + jnp.arange(window, dtype=jnp.int32)
        key_docs = lax.dynamic_slice_in_dim(key_doc, win0, window)
        q_pos = lax.dynamic_slice_in_dim(position, row0, BLK)
        q_docs = lax.dynamic_slice_in_dim(query_doc, row0, BLK)
        allowed = (q_docs[:, None] == key_docs[None, :]) & (key_pos[None, :] <= q_pos[:, None])
        scores = jnp.einsum("qghd,kgd->qghk", q_tile, key_win) * scale
        probs = jnp.where(allowed[:, None, None, :], jnp.exp(scores - lse_tile[..., None]), jnp.float32(0.0))
        probs_low = lax.optimization_barrier(probs.astype(jnp.bfloat16)).astype(jnp.float32)
        value_part = jnp.einsum("qghk,qghd->kgd", probs_low, do_tile)
        dprob = jnp.einsum("qghd,kgd->qghk", do_tile, value_win)
        dscore = lax.optimization_barrier((probs * (dprob - delta_tile[..., None])).astype(jnp.bfloat16)).astype(jnp.float32)
        grad_q = (jnp.einsum("qghk,kgd->qghd", dscore, key_win) * scale).astype(jnp.bfloat16)
        key_part = jnp.einsum("qghk,qghd->kgd", dscore, q_tile) * scale
        key_total = lax.dynamic_update_slice_in_dim(key_total, lax.dynamic_slice_in_dim(key_total, win0, window) + key_part, win0, 0)
        value_total = lax.dynamic_update_slice_in_dim(value_total, lax.dynamic_slice_in_dim(value_total, win0, window) + value_part, win0, 0)
        return (key_total, value_total), grad_q

    start = (jnp.zeros((S, KVH, DH), jnp.float32), jnp.zeros((S, KVH, DH), jnp.float32))
    (key_total, value_total), grad_q = lax.scan(step, start, jnp.arange(NB, dtype=jnp.int32))
    grad_queries = grad_q.reshape(S, H, DH)
    grad_keys = key_total.reshape(S, KVH * DH).astype(jnp.bfloat16)
    grad_values = value_total.reshape(S, KVH * DH).astype(jnp.bfloat16)
    return (grad_queries, grad_keys, grad_values)
```

```python
import functools

import jax
import jax.numpy as jnp
from jax import lax
from jax.experimental import pallas as pl
from jax.experimental.pallas import tpu as pltpu
from jax.sharding import Mesh
from jax.sharding import PartitionSpec as P

BLK = 128
WIN = 5
ZL, NY, NCORE, NX, ZH = 4, 4, 2, 4, 2
LOG2E = 1.4426950408889634


def attention_kernel(
    info, ends, q_ref, do_ref, stats_ref, kv0, kv1, kv2, kv3,
    dq_ref, p0_ref, p1_ref, p2_ref, p3_ref,
    win_ref, kt_ref, acc_ref,
    *, chunk, group,
):
    rows, dh = q_ref.shape
    scale = dh ** (-0.5)
    q_block = info[0]
    slots = (kv0, kv1, kv2, kv3)
    outs = (p0_ref, p1_ref, p2_ref, p3_ref)
    for w in range(WIN):
        slot = info[1 + w]
        for s in range(4):
            for i in range(2):
                @pl.when(slot == 2 * s + i)
                def _():
                    win_ref[w * BLK : (w + 1) * BLK, :] = slots[s][i]
    kt_ref[...] = win_ref[:, :dh].T
    acc_ref[...] = jnp.zeros_like(acc_ref)

    def step(c, carry):
        at = pl.multiple_of(c * chunk, chunk)
        q = q_ref[pl.ds(at, chunk), :]
        do = do_ref[pl.ds(at, chunk), :]
        lse = stats_ref[0:1, pl.ds(at, chunk)]
        delta = stats_ref[1:2, pl.ds(at, chunk)]
        pos = q_block * BLK + (at + lax.broadcasted_iota(jnp.int32, (1, chunk), 1)) // group
        start = jnp.zeros((1, chunk), jnp.int32)
        for k in range(ends.shape[0]):
            start = jnp.where(ends[k] <= pos, ends[k], start)
        key_pos = (q_block - (WIN - 1)) * BLK + lax.broadcasted_iota(
            jnp.int32, (WIN * BLK, chunk), 0
        )
        allowed = (key_pos >= start) & (key_pos <= pos)
        keys = win_ref[:, :dh]
        vals = win_ref[:, dh:]
        nt = (((1,), (1,)), ((), ()))
        s = lax.dot_general(keys, q, nt, preferred_element_type=jnp.float32)
        p = jnp.where(allowed, jnp.exp2(s * (scale * LOG2E) - lse), 0.0)
        dp = lax.dot_general(vals, do, nt, preferred_element_type=jnp.float32)
        ds = (p * (dp - delta)).astype(jnp.bfloat16)
        acc_ref[:, dh:] += jnp.dot(p.astype(jnp.bfloat16), do, preferred_element_type=jnp.float32)
        acc_ref[:, :dh] += jnp.dot(ds, q, preferred_element_type=jnp.float32)
        dqt = jnp.dot(kt_ref[...], ds, preferred_element_type=jnp.float32)
        dq_ref[pl.ds(at, chunk), :] = (dqt * scale).T.astype(dq_ref.dtype)
        return carry

    lax.fori_loop(0, rows // chunk, step, 0)
    acc_ref[:, :dh] = acc_ref[:, :dh] * scale
    for s in range(4):
        for i in range(2):
            w = info[6 + 2 * s + i]

            @pl.when(w >= 0)
            def _():
                at = pl.multiple_of(jnp.maximum(w, 0) * BLK, BLK)
                outs[s][i] = acc_ref[pl.ds(at, BLK), :].astype(outs[s].dtype)

            @pl.when(w < 0)
            def _():
                outs[s][i] = jnp.zeros((BLK, 2 * dh), outs[s].dtype)


def attention(info, ends, q, do, stats, kvs):
    rows, dh = q.shape
    part = (2, BLK, 2 * dh)
    smem = pl.BlockSpec(memory_space=pltpu.SMEM)
    vmem = pl.BlockSpec(memory_space=pltpu.VMEM)
    return pl.pallas_call(
        functools.partial(attention_kernel, chunk=256, group=rows // BLK),
        out_shape=(
            jax.ShapeDtypeStruct((rows, dh), jnp.bfloat16),
            jax.ShapeDtypeStruct(part, jnp.float32),
            jax.ShapeDtypeStruct(part, jnp.bfloat16),
            jax.ShapeDtypeStruct(part, jnp.bfloat16),
            jax.ShapeDtypeStruct(part, jnp.bfloat16),
        ),
        in_specs=[smem, smem] + [vmem] * 7,
        out_specs=(vmem,) * 5,
        scratch_shapes=[
            pltpu.VMEM((WIN * BLK, 2 * dh), jnp.bfloat16),
            pltpu.VMEM((dh, WIN * BLK), jnp.bfloat16),
            pltpu.VMEM((WIN * BLK, 2 * dh), jnp.float32),
        ],
        compiler_params=pltpu.CompilerParams(vmem_limit_bytes=40 * 1024 * 1024),
        cost_estimate=pl.CostEstimate(
            flops=10 * rows * WIN * BLK * dh, bytes_accessed=4 * rows * dh * 2, transcendentals=rows * WIN * BLK
        ),
        name="attention_backward",
    )(info, ends, q, do, stats, *kvs)


def swap(x, axis, size, mask):
    return lax.ppermute(x, axis, [(i, i ^ mask) for i in range(size)])


def local(queries, keys, values, outputs, out_grad, logsumexp, doc_lengths, block_order):
    rows, heads, dh = queries.shape
    zl = lax.axis_index("zl")
    y = lax.axis_index("y")
    core = lax.axis_index("core")
    ends = jnp.cumsum(doc_lengths).astype(jnp.int32)
    xor4 = jnp.arange(4, dtype=jnp.int32)

    own = jnp.concatenate([keys[:, 0, :], values[:, 0, :]], axis=1)
    column = jnp.stack([own] + [swap(own, "zl", ZL, m) for m in (1, 2, 3)])
    other = swap(column, "core", NCORE, 1)
    pairs = jnp.stack([column, other], axis=1)

    order = block_order.reshape(ZL, NY, NCORE)
    near = order[zl, y ^ xor4, core]
    first = jnp.maximum(near // 2 - 2, 0)
    want = jnp.minimum(first + (y - first) % 4, 15) // 4
    sends = [lax.dynamic_index_in_dim(pairs, zl ^ want[m], 0, keepdims=False) for m in range(4)]
    got = [sends[0]] + [swap(sends[m], "y", NY, m) for m in (1, 2, 3)]

    q_block = near[0]
    win = jnp.maximum(q_block - (WIN - 1) + jnp.arange(WIN, dtype=jnp.int32), 0)
    slot = (((win // 2) % 4) ^ y) * 2 + ((win % 2) ^ core)
    cls = y ^ xor4
    pair_of = first[0] + (cls - first[0]) % 4
    block_of = pair_of[:, None] * 2 + (core ^ jnp.arange(2, dtype=jnp.int32))[None, :]
    place = block_of - (q_block - (WIN - 1))
    usable = (place >= 0) & (place < WIN) & (block_of >= 0)
    place = jnp.where(usable, place, -1).reshape(-1)
    info = jnp.concatenate([q_block[None], slot, place]).astype(jnp.int32)

    delta = jnp.sum(out_grad.astype(jnp.float32) * outputs.astype(jnp.float32), axis=2)
    stats = jnp.stack([(logsumexp * LOG2E).T.reshape(-1), delta.reshape(-1)])
    grad_q, part0, part1, part2, part3 = attention(
        info, ends, queries.reshape(rows * heads, dh), out_grad.reshape(rows * heads, dh), stats, got
    )

    parts = [part0] + [swap(p, "y", NY, m) for m, p in ((1, part1), (2, part2), (3, part3))]
    total = sum(
        jnp.where((want[m] == xor4)[:, None, None, None], parts[m].astype(jnp.float32)[None], 0.0)
        for m in range(4)
    )
    theirs = swap(total[:, 1].astype(jnp.bfloat16), "core", NCORE, 1)
    mine = (total[:, 0] + theirs.astype(jnp.float32)).astype(jnp.bfloat16)
    kvh = NX * ZH
    share = BLK // kvh
    moved = lax.all_to_all(
        mine.reshape(ZL * kvh, share, 2 * dh), ("zl", "x", "zh"), split_axis=0, concat_axis=0, tiled=True
    )
    summed = jnp.sum(moved.reshape(ZL, kvh, share, 2 * dh).astype(jnp.float32), axis=0)
    grads = jnp.transpose(summed.astype(jnp.bfloat16), (1, 0, 2))
    grad_keys = grads[:, :, :dh].reshape(share, kvh * dh)
    grad_values = grads[:, :, dh:].reshape(share, kvh * dh)
    return grad_q.reshape(rows, heads, dh), grad_keys, grad_values


def solution(mesh):
    fine = Mesh(mesh.devices.reshape(ZL, NY, NCORE, NX, ZH), ("zl", "y", "core", "x", "zh"))
    ctx, kv = ("zl", "y", "core"), ("x", "zh")
    in_specs = (P(ctx, kv, None),) * 5 + (P(kv, ctx), P(), P())
    out_specs = (P(ctx, kv, None), P(ctx + kv, None), P(ctx + kv, None))
    return jax.shard_map(local, mesh=fine, in_specs=in_specs, out_specs=out_specs, check_vma=False)
```

```python
import functools

import jax
import jax.numpy as jnp
from jax import lax
from jax.experimental import pallas as pl
from jax.experimental.pallas import tpu as pltpu
from jax.sharding import Mesh
from jax.sharding import PartitionSpec as P

BLK = 128
WIN = 5
ZL, NY, NCORE, NX, ZH = 4, 4, 2, 4, 2
KVH = NX * ZH
LOG2E = 1.4426950408889634
CHUNK = 1024
LANES = 128
SEND, WANT, BASE0, BASE1, ACTIVE = 0, 4, 8, 12, 16
NT = (((1,), (1,)), ((), ()))
TN = (((0,), (0,)), ((), ()))
SMEM = pl.BlockSpec(memory_space=pltpu.SMEM)
VMEM = pl.BlockSpec(memory_space=pltpu.VMEM)


def call(body, outs, inputs, name, scratch=(), specs=None, flops=0, moved=1 << 18):
    return pl.pallas_call(
        body,
        out_shape=outs,
        in_specs=specs or [VMEM] * len(inputs),
        out_specs=jax.tree.map(lambda _: VMEM, outs),
        scratch_shapes=scratch,
        compiler_params=pltpu.CompilerParams(vmem_limit_bytes=16 * 1024 * 1024),
        cost_estimate=pl.CostEstimate(flops=flops, bytes_accessed=moved, transcendentals=0),
        name=name,
    )(*inputs)


def plan_kernel(order, lengths, plan_ref, span_ref, *, group):
    zl, y, core = lax.axis_index("zl"), lax.axis_index("y"), lax.axis_index("core")
    ends, total = [], 0
    for k in range(lengths.shape[0]):
        total = total + lengths[k]
        ends.append(total)

    def put(row, value):
        plan_ref[row : row + 1, :] = jnp.full((1, LANES), value, jnp.int32)

    me = order[(zl * NY + y) * NCORE + core]
    q_first = me * BLK
    doc_first = 0
    for end in ends:
        doc_first = jnp.where(end <= q_first, end, doc_first)
    mine = jnp.maximum(lax.shift_right_logical(me, 1) - 2, 0)
    for m in range(4):
        near = order[(zl * NY + (y ^ m)) * NCORE + core]
        first = jnp.maximum(lax.shift_right_logical(near, 1) - 2, 0)
        pair = jnp.minimum(first + ((y - first) & 3), 15)
        want = lax.shift_right_logical(pair, 2)
        put(SEND + m, zl ^ want)
        put(WANT + m, want)
        offset = ((y ^ m) - mine) & 3
        low = (mine + offset) * (2 * BLK)
        put(BASE0 + m, low + core * BLK)
        put(BASE1 + m, low + (1 - core) * BLK)
        active = (offset < 3) & (low < q_first + BLK) & (low + 2 * BLK > doc_first)
        put(ACTIVE + m, active.astype(jnp.int32))
    cols = span_ref.shape[1]
    pos = q_first + lax.broadcasted_iota(jnp.int32, (1, cols), 1) // group
    start = jnp.zeros((1, cols), jnp.int32)
    for end in ends:
        start = jnp.where(end <= pos, end, start)
    span_ref[0:1, :] = start
    span_ref[1:2, :] = pos


def select_kernel(plan, own, col1, col2, col3, theirs, *outs):
    mine = (own, col1, col2, col3)
    for m in range(4):
        at = jnp.concatenate([plan[SEND + m : SEND + m + 1, :]] * (own.shape[1] // LANES), axis=1)
        one, two = mine[0][...], theirs[0]
        for s in range(1, 4):
            one = jnp.where(at == s, mine[s][...], one)
            two = jnp.where(at == s, theirs[s], two)
        outs[m][:BLK, :] = one
        outs[m][BLK:, :] = two


def class_kernel(plan, q_ref, do_ref, stats, span, kv, part_ref, ds_ref, acc, *, m):
    rows, dh = q_ref.shape
    keys = kv.shape[0]
    scale = dh ** (-0.5)
    active = jnp.max(plan[ACTIVE + m : ACTIVE + m + 1, :]) > 0

    @pl.when(jnp.logical_not(active))
    def _():
        part_ref[...] = jnp.zeros_like(part_ref)

    @pl.when(active)
    def _():
        acc[...] = jnp.zeros_like(acc)
        row = lax.broadcasted_iota(jnp.int32, (BLK, 1), 0)
        key_pos = jnp.concatenate(
            [row + plan[BASE0 + m : BASE0 + m + 1, 0:1], row + plan[BASE1 + m : BASE1 + m + 1, 0:1]], axis=0
        )

        def step(c, carry):
            at = pl.multiple_of(c * CHUNK, CHUNK)
            cols = pl.ds(at, CHUNK)
            q = q_ref[cols, :]
            do = do_ref[cols, :]
            allowed = (key_pos >= span[0:1, cols]) & (key_pos <= span[1:2, cols])
            s = lax.dot_general(kv[:, :dh], q, NT, preferred_element_type=jnp.float32)
            p = jnp.where(allowed, jnp.exp2(s * (scale * LOG2E) - stats[0:1, cols]), 0.0)
            dp = lax.dot_general(kv[:, dh:], do, NT, preferred_element_type=jnp.float32)
            ds = (p * (dp - stats[1:2, cols])).astype(jnp.bfloat16)
            acc[:, dh:] += jnp.dot(p.astype(jnp.bfloat16), do, preferred_element_type=jnp.float32)
            acc[:, :dh] += jnp.dot(ds, q, preferred_element_type=jnp.float32)
            ds_ref[:, cols] = ds
            return carry

        lax.fori_loop(0, rows // CHUNK, step, 0)
        part_ref[:, :dh] = (acc[:, :dh] * scale).astype(part_ref.dtype)
        part_ref[:, dh:] = acc[:, dh:].astype(part_ref.dtype)


def query_kernel(plan, kv0, kv1, kv2, kv3, ds0, ds1, ds2, ds3, dq_ref, acc):
    rows, dh = dq_ref.shape
    acc[...] = jnp.zeros_like(acc)
    for m, (kv, ds) in enumerate(((kv0, ds0), (kv1, ds1), (kv2, ds2), (kv3, ds3))):

        @pl.when(jnp.max(plan[ACTIVE + m : ACTIVE + m + 1, :]) > 0)
        def _():
            def step(c, carry):
                cols = pl.ds(pl.multiple_of(c * CHUNK, CHUNK), CHUNK)
                acc[:, cols] += lax.dot_general(
                    kv[:, :dh], ds[:, cols], TN, preferred_element_type=jnp.float32
                )
                return carry

            lax.fori_loop(0, rows // CHUNK, step, 0)

    def finish(c, carry):
        cols = pl.ds(pl.multiple_of(c * CHUNK, CHUNK), CHUNK)
        dq_ref[cols, :] = (acc[:, cols] * dh ** (-0.5)).T.astype(dq_ref.dtype)
        return carry

    lax.fori_loop(0, rows // CHUNK, finish, 0)


def total_kernel(plan, part0, part1, part2, part3, keep_ref, send_ref):
    parts = (part0, part1, part2, part3)
    wide = part0.shape[1] // LANES
    wants = [jnp.concatenate([plan[WANT + m : WANT + m + 1, :]] * wide, axis=1) for m in range(4)]
    for z in range(ZL):
        keep = jnp.zeros((BLK, wide * LANES), jnp.float32)
        send = jnp.zeros((BLK, wide * LANES), jnp.float32)
        for m in range(4):
            here = wants[m] == z
            keep += jnp.where(here, parts[m][:BLK, :].astype(jnp.float32), 0.0)
            send += jnp.where(here, parts[m][BLK:, :].astype(jnp.float32), 0.0)
        keep_ref[z] = keep
        send_ref[z] = send.astype(send_ref.dtype)


def finish_kernel(moved, gk_ref, gv_ref):
    dh = moved.shape[2] // 2
    for k in range(KVH):
        grad = moved[k].astype(jnp.float32)
        for z in range(1, ZL):
            grad += moved[z * KVH + k].astype(jnp.float32)
        gk_ref[:, k * dh : (k + 1) * dh] = grad[:, :dh].astype(gk_ref.dtype)
        gv_ref[:, k * dh : (k + 1) * dh] = grad[:, dh:].astype(gv_ref.dtype)


def swap(x, axis, size, mask):
    return lax.ppermute(x, axis, [(i, i ^ mask) for i in range(size)])


def local(queries, keys, values, outputs, out_grad, logsumexp, doc_lengths, block_order):
    rows, heads, dh = queries.shape
    cols = rows * heads
    wide = 2 * dh
    bf16, f32 = jnp.bfloat16, jnp.float32
    shape = jax.ShapeDtypeStruct

    own = jnp.concatenate([keys[:, 0, :], values[:, 0, :]], axis=1)
    column = [own] + [swap(own, "zl", ZL, m) for m in (1, 2, 3)]
    plan, span = call(
        functools.partial(plan_kernel, group=heads),
        (shape((24, LANES), jnp.int32), shape((2, cols), jnp.int32)),
        (block_order, doc_lengths), "plan", specs=[SMEM, SMEM],
    )
    delta = jnp.sum(out_grad.astype(f32) * outputs.astype(f32), axis=2)
    stats = jnp.stack([(logsumexp * LOG2E).T.reshape(-1), delta.reshape(-1)])
    q = queries.reshape(cols, dh)
    do = out_grad.reshape(cols, dh)
    theirs = swap(jnp.stack(column), "core", NCORE, 1)

    pair = shape((2 * BLK, wide), bf16)
    sends = call(select_kernel, (pair,) * 4, (plan, *column, theirs), "select")
    kvs, parts, dss = [None] * 4, [None] * 4, [None] * 4
    kvs[0] = sends[0]
    for m in (1, 3, 2):
        kvs[m] = swap(sends[m], "y", NY, m)
    for m in (0, 1, 3, 2):
        parts[m], dss[m] = call(
            functools.partial(class_kernel, m=m),
            (shape((2 * BLK, wide), f32 if m == 0 else bf16), shape((2 * BLK, cols), bf16)),
            (plan, q, do, stats, span, kvs[m]), "class" + str(m),
            scratch=[pltpu.VMEM((2 * BLK, wide), f32)],
            flops=8 * cols * 2 * BLK * dh, moved=3 * cols * dh * 2,
        )
    back = [parts[0]] + [swap(parts[m], "y", NY, m) for m in (1, 2, 3)]
    grad_q = call(
        query_kernel, shape((cols, dh), bf16), (plan, *kvs, *dss), "query",
        scratch=[pltpu.VMEM((dh, cols), f32)], flops=8 * cols * 2 * BLK * dh, moved=8 * cols * dh * 2,
    )

    keep, send = call(
        total_kernel, (shape((ZL, BLK, wide), f32), shape((ZL, BLK, wide), bf16)), (plan, *back), "total"
    )
    mine = (keep + swap(send, "core", NCORE, 1).astype(f32)).astype(bf16)
    share = BLK // KVH
    moved = lax.all_to_all(
        mine.reshape(ZL * KVH, share, wide), ("zl", "x", "zh"), split_axis=0, concat_axis=0, tiled=True
    )
    out = shape((share, KVH * dh), bf16)
    grad_keys, grad_values = call(finish_kernel, (out, out), (moved,), "finish")
    return grad_q.reshape(rows, heads, dh), grad_keys, grad_values


def solution(mesh):
    fine = Mesh(mesh.devices.reshape(ZL, NY, NCORE, NX, ZH), ("zl", "y", "core", "x", "zh"))
    ctx, kv = ("zl", "y", "core"), ("x", "zh")
    in_specs = (P(ctx, kv, None),) * 5 + (P(kv, ctx), P(), P())
    out_specs = (P(ctx, kv, None), P(ctx + kv, None), P(ctx + kv, None))
    return jax.shard_map(local, mesh=fine, in_specs=in_specs, out_specs=out_specs, check_vma=False)
```

```python
import functools

import jax
import jax.numpy as jnp
from jax import lax
from jax.experimental import pallas as pl
from jax.experimental.pallas import tpu as pltpu
from jax.sharding import Mesh
from jax.sharding import PartitionSpec as P

BLK = 128
WIN = 5
ZL, NY, NCORE, NX, ZH = 4, 4, 2, 4, 2
KVH = NX * ZH
LOG2E = 1.4426950408889634
CHUNK = 1024
LANES = 128
SEND, WANT, BASE0, BASE1, ACTIVE = 0, 4, 8, 12, 16
NT = (((1,), (1,)), ((), ()))
TN = (((0,), (0,)), ((), ()))
SMEM = pl.BlockSpec(memory_space=pltpu.SMEM)
VMEM = pl.BlockSpec(memory_space=pltpu.VMEM)


def call(body, outs, inputs, name, scratch=(), specs=None, flops=0, moved=1 << 18):
    return pl.pallas_call(
        body,
        out_shape=outs,
        in_specs=specs or [VMEM] * len(inputs),
        out_specs=jax.tree.map(lambda _: VMEM, outs),
        scratch_shapes=scratch,
        compiler_params=pltpu.CompilerParams(vmem_limit_bytes=16 * 1024 * 1024),
        cost_estimate=pl.CostEstimate(flops=flops, bytes_accessed=moved, transcendentals=0),
        name=name,
    )(*inputs)


def plan_kernel(order, lengths, plan_ref, span_ref, *, group):
    zl, y, core = lax.axis_index("zl"), lax.axis_index("y"), lax.axis_index("core")
    ends, total = [], 0
    for k in range(lengths.shape[0]):
        total = total + lengths[k]
        ends.append(total)

    def put(row, value):
        plan_ref[row : row + 1, :] = jnp.full((1, LANES), value, jnp.int32)

    me = order[(zl * NY + y) * NCORE + core]
    q_first = me * BLK
    doc_first = 0
    for end in ends:
        doc_first = jnp.where(end <= q_first, end, doc_first)
    mine = jnp.maximum(lax.shift_right_logical(me, 1) - 2, 0)
    for m in range(4):
        near = order[(zl * NY + (y ^ m)) * NCORE + core]
        first = jnp.maximum(lax.shift_right_logical(near, 1) - 2, 0)
        pair = jnp.minimum(first + ((y - first) & 3), 15)
        want = lax.shift_right_logical(pair, 2)
        put(SEND + m, zl ^ want)
        put(WANT + m, want)
        offset = ((y ^ m) - mine) & 3
        low = (mine + offset) * (2 * BLK)
        put(BASE0 + m, low + core * BLK)
        put(BASE1 + m, low + (1 - core) * BLK)
        active = (offset < 3) & (low < q_first + BLK) & (low + 2 * BLK > doc_first)
        put(ACTIVE + m, active.astype(jnp.int32))
    cols = span_ref.shape[1]
    pos = q_first + lax.broadcasted_iota(jnp.int32, (1, cols), 1) // group
    start = jnp.zeros((1, cols), jnp.int32)
    for end in ends:
        start = jnp.where(end <= pos, end, start)
    span_ref[0:1, :] = start
    span_ref[1:2, :] = pos


def stack_kernel(own, col1, col2, col3, plan, span, stats, out, token):
    for s, ref in enumerate((own, col1, col2, col3)):
        out[s] = ref[...]
    token[...] = jnp.zeros_like(token)


def add_kernel(keep, theirs, out):
    out[...] = (keep[...] + theirs[...].astype(jnp.float32)).astype(out.dtype)


def select_kernel(plan, own, col1, col2, col3, theirs, *outs):
    mine = (own, col1, col2, col3)
    for m in range(4):
        at = jnp.concatenate([plan[SEND + m : SEND + m + 1, :]] * (own.shape[1] // LANES), axis=1)
        one, two = mine[0][...], theirs[0]
        for s in range(1, 4):
            one = jnp.where(at == s, mine[s][...], one)
            two = jnp.where(at == s, theirs[s], two)
        outs[m][:BLK, :] = one
        outs[m][BLK:, :] = two


def class_kernel(plan, q_ref, do_ref, stats, span, kv, before, part_ref, ds_ref, after, acc, *, m):
    rows, dh = q_ref.shape
    keys = kv.shape[0]
    scale = dh ** (-0.5)
    active = jnp.max(plan[ACTIVE + m : ACTIVE + m + 1, :]) > 0
    after[...] = before[...]

    @pl.when(jnp.logical_not(active))
    def _():
        part_ref[...] = jnp.zeros_like(part_ref)

    @pl.when(active)
    def _():
        acc[...] = jnp.zeros_like(acc)
        row = lax.broadcasted_iota(jnp.int32, (BLK, 1), 0)
        key_pos = jnp.concatenate(
            [row + plan[BASE0 + m : BASE0 + m + 1, 0:1], row + plan[BASE1 + m : BASE1 + m + 1, 0:1]], axis=0
        )

        def step(c, carry):
            at = pl.multiple_of(c * CHUNK, CHUNK)
            cols = pl.ds(at, CHUNK)
            q = q_ref[cols, :]
            do = do_ref[cols, :]
            allowed = (key_pos >= span[0:1, cols]) & (key_pos <= span[1:2, cols])
            s = lax.dot_general(kv[:, :dh], q, NT, preferred_element_type=jnp.float32)
            p = jnp.where(allowed, jnp.exp2(s * (scale * LOG2E) - stats[0:1, cols]), 0.0)
            dp = lax.dot_general(kv[:, dh:], do, NT, preferred_element_type=jnp.float32)
            ds = (p * (dp - stats[1:2, cols])).astype(jnp.bfloat16)
            acc[:, dh:] += jnp.dot(p.astype(jnp.bfloat16), do, preferred_element_type=jnp.float32)
            acc[:, :dh] += jnp.dot(ds, q, preferred_element_type=jnp.float32)
            ds_ref[:, cols] = ds
            return carry

        lax.fori_loop(0, rows // CHUNK, step, 0)
        part_ref[:, :dh] = (acc[:, :dh] * scale).astype(part_ref.dtype)
        part_ref[:, dh:] = acc[:, dh:].astype(part_ref.dtype)


def query_kernel(plan, kv0, kv1, kv2, kv3, ds0, ds1, ds2, ds3, before, dq_ref, after, acc):
    rows, dh = dq_ref.shape
    after[...] = before[...]
    acc[...] = jnp.zeros_like(acc)
    for m, (kv, ds) in enumerate(((kv0, ds0), (kv1, ds1), (kv2, ds2), (kv3, ds3))):

        @pl.when(jnp.max(plan[ACTIVE + m : ACTIVE + m + 1, :]) > 0)
        def _():
            def step(c, carry):
                cols = pl.ds(pl.multiple_of(c * CHUNK, CHUNK), CHUNK)
                acc[:, cols] += lax.dot_general(
                    kv[:, :dh], ds[:, cols], TN, preferred_element_type=jnp.float32
                )
                return carry

            lax.fori_loop(0, rows // CHUNK, step, 0)

    def finish(c, carry):
        cols = pl.ds(pl.multiple_of(c * CHUNK, CHUNK), CHUNK)
        dq_ref[cols, :] = (acc[:, cols] * dh ** (-0.5)).T.astype(dq_ref.dtype)
        return carry

    lax.fori_loop(0, rows // CHUNK, finish, 0)


def total_kernel(plan, part0, part1, part2, part3, before, keep_ref, send_ref):
    parts = (part0, part1, part2, part3)
    wide = part0.shape[1] // LANES
    wants = [jnp.concatenate([plan[WANT + m : WANT + m + 1, :]] * wide, axis=1) for m in range(4)]
    for z in range(ZL):
        keep = jnp.zeros((BLK, wide * LANES), jnp.float32)
        send = jnp.zeros((BLK, wide * LANES), jnp.float32)
        for m in range(4):
            here = wants[m] == z
            keep += jnp.where(here, parts[m][:BLK, :].astype(jnp.float32), 0.0)
            send += jnp.where(here, parts[m][BLK:, :].astype(jnp.float32), 0.0)
        keep_ref[z] = keep
        send_ref[z] = send.astype(send_ref.dtype)


def finish_kernel(moved, gk_ref, gv_ref):
    dh = moved.shape[2] // 2
    for k in range(KVH):
        grad = moved[k].astype(jnp.float32)
        for z in range(1, ZL):
            grad += moved[z * KVH + k].astype(jnp.float32)
        gk_ref[:, k * dh : (k + 1) * dh] = grad[:, :dh].astype(gk_ref.dtype)
        gv_ref[:, k * dh : (k + 1) * dh] = grad[:, dh:].astype(gv_ref.dtype)


def swap(x, axis, size, mask):
    return lax.ppermute(x, axis, [(i, i ^ mask) for i in range(size)])


def local(queries, keys, values, outputs, out_grad, logsumexp, doc_lengths, block_order):
    rows, heads, dh = queries.shape
    cols = rows * heads
    wide = 2 * dh
    bf16, f32 = jnp.bfloat16, jnp.float32
    shape = jax.ShapeDtypeStruct

    own = jnp.concatenate([keys[:, 0, :], values[:, 0, :]], axis=1)
    column = [own] + [swap(own, "zl", ZL, m) for m in (1, 2, 3)]
    plan, span = call(
        functools.partial(plan_kernel, group=heads),
        (shape((24, LANES), jnp.int32), shape((2, cols), jnp.int32)),
        (block_order, doc_lengths), "plan", specs=[SMEM, SMEM],
    )
    delta = jnp.sum(out_grad.astype(f32) * outputs.astype(f32), axis=2)
    stats = jnp.stack([(logsumexp * LOG2E).T.reshape(-1), delta.reshape(-1)])
    q = queries.reshape(cols, dh)
    do = out_grad.reshape(cols, dh)
    stacked, token = call(
        stack_kernel, (shape((4, BLK, wide), bf16), shape((8, LANES), f32)),
        (*column, plan, span, stats), "stacked",
    )
    theirs = swap(stacked, "core", NCORE, 1)

    pair = shape((2 * BLK, wide), bf16)
    sends = call(select_kernel, (pair,) * 4, (plan, *column, theirs), "select")
    kvs = [sends[0]] + [swap(sends[m], "y", NY, m) for m in (1, 2, 3)]
    parts, dss = [], []
    for m in range(4):
        part, ds, token = call(
            functools.partial(class_kernel, m=m),
            (shape((2 * BLK, wide), f32 if m == 0 else bf16), shape((2 * BLK, cols), bf16), shape((8, LANES), f32)),
            (plan, q, do, stats, span, kvs[m], token), "class" + str(m),
            scratch=[pltpu.VMEM((2 * BLK, wide), f32)],
            flops=8 * cols * 2 * BLK * dh, moved=3 * cols * dh * 2,
        )
        parts.append(part)
        dss.append(ds)
    back = [parts[0]] + [swap(parts[m], "y", NY, m) for m in (1, 2, 3)]
    grad_q, token = call(
        query_kernel, (shape((cols, dh), bf16), shape((8, LANES), f32)), (plan, *kvs, *dss, token), "query",
        scratch=[pltpu.VMEM((dh, cols), f32)], flops=8 * cols * 2 * BLK * dh, moved=8 * cols * dh * 2,
    )

    keep, send = call(
        total_kernel, (shape((ZL, BLK, wide), f32), shape((ZL, BLK, wide), bf16)), (plan, *back, token), "total"
    )
    mine = call(add_kernel, shape((ZL, BLK, wide), bf16), (keep, swap(send, "core", NCORE, 1)), "add")
    share = BLK // KVH
    moved = lax.all_to_all(
        mine.reshape(ZL * KVH, share, wide), ("zl", "x", "zh"), split_axis=0, concat_axis=0, tiled=True
    )
    out = shape((share, KVH * dh), bf16)
    grad_keys, grad_values = call(finish_kernel, (out, out), (moved,), "finish")
    return grad_q.reshape(rows, heads, dh), grad_keys, grad_values


def solution(mesh):
    fine = Mesh(mesh.devices.reshape(ZL, NY, NCORE, NX, ZH), ("zl", "y", "core", "x", "zh"))
    ctx, kv = ("zl", "y", "core"), ("x", "zh")
    in_specs = (P(ctx, kv, None),) * 5 + (P(kv, ctx), P(), P())
    out_specs = (P(ctx, kv, None), P(ctx + kv, None), P(ctx + kv, None))
    return jax.shard_map(local, mesh=fine, in_specs=in_specs, out_specs=out_specs, check_vma=False)
```

```python
import functools

import jax
import jax.numpy as jnp
from jax import lax
from jax.experimental import pallas as pl
from jax.experimental.pallas import tpu as pltpu
from jax.sharding import Mesh
from jax.sharding import PartitionSpec as P

BLK = 128
WIN = 5
ZL, NY, NCORE, NX, ZH = 4, 4, 2, 4, 2
KVH = NX * ZH
LOG2E = 1.4426950408889634
CHUNK = 1024
LANES = 128
SEND, WANT, BASE0, BASE1, ACTIVE = 0, 4, 8, 12, 16
NT = (((1,), (1,)), ((), ()))
TN = (((0,), (0,)), ((), ()))
SMEM = pl.BlockSpec(memory_space=pltpu.SMEM)
VMEM = pl.BlockSpec(memory_space=pltpu.VMEM)


def call(body, outs, inputs, name, scratch=(), specs=None, flops=0, moved=1 << 18):
    return pl.pallas_call(
        body,
        out_shape=outs,
        in_specs=specs or [VMEM] * len(inputs),
        out_specs=jax.tree.map(lambda _: VMEM, outs),
        scratch_shapes=scratch,
        compiler_params=pltpu.CompilerParams(vmem_limit_bytes=16 * 1024 * 1024),
        cost_estimate=pl.CostEstimate(flops=flops, bytes_accessed=moved, transcendentals=0),
        name=name,
    )(*inputs)


def plan_kernel(order, lengths, plan_ref, span_ref, *, group):
    zl, y, core = lax.axis_index("zl"), lax.axis_index("y"), lax.axis_index("core")
    ends, total = [], 0
    for k in range(lengths.shape[0]):
        total = total + lengths[k]
        ends.append(total)

    def put(row, value):
        plan_ref[row : row + 1, :] = jnp.full((1, LANES), value, jnp.int32)

    me = order[(zl * NY + y) * NCORE + core]
    q_first = me * BLK
    doc_first = 0
    for end in ends:
        doc_first = jnp.where(end <= q_first, end, doc_first)
    mine = jnp.maximum(lax.shift_right_logical(me, 1) - 2, 0)
    for m in range(4):
        near = order[(zl * NY + (y ^ m)) * NCORE + core]
        first = jnp.maximum(lax.shift_right_logical(near, 1) - 2, 0)
        pair = jnp.minimum(first + ((y - first) & 3), 15)
        want = lax.shift_right_logical(pair, 2)
        put(SEND + m, zl ^ want)
        put(WANT + m, want)
        offset = ((y ^ m) - mine) & 3
        low = (mine + offset) * (2 * BLK)
        put(BASE0 + m, low + core * BLK)
        put(BASE1 + m, low + (1 - core) * BLK)
        active = (offset < 3) & (low < q_first + BLK) & (low + 2 * BLK > doc_first)
        put(ACTIVE + m, active.astype(jnp.int32))
    cols = span_ref.shape[1]
    pos = q_first + lax.broadcasted_iota(jnp.int32, (1, cols), 1) // group
    start = jnp.zeros((1, cols), jnp.int32)
    for end in ends:
        start = jnp.where(end <= pos, end, start)
    span_ref[0:1, :] = start
    span_ref[1:2, :] = pos


def stack_kernel(own, col1, col2, col3, plan, span, stats, out, token):
    for s, ref in enumerate((own, col1, col2, col3)):
        out[s] = ref[...]
    token[...] = jnp.zeros_like(token)


def add_kernel(keep, theirs, out):
    out[...] = (keep[...] + theirs[...].astype(jnp.float32)).astype(out.dtype)


def select_kernel(plan, own, col1, col2, col3, theirs, *outs):
    mine = (own, col1, col2, col3)
    for m in range(4):
        at = jnp.concatenate([plan[SEND + m : SEND + m + 1, :]] * (own.shape[1] // LANES), axis=1)
        one, two = mine[0][...], theirs[0]
        for s in range(1, 4):
            one = jnp.where(at == s, mine[s][...], one)
            two = jnp.where(at == s, theirs[s], two)
        outs[m][:BLK, :] = one
        outs[m][BLK:, :] = two


def class_kernel(plan, q_ref, do_ref, stats, span, kv, before, part_ref, ds_ref, after, acc, *, m):
    rows, dh = q_ref.shape
    keys = kv.shape[0]
    scale = dh ** (-0.5)
    active = jnp.max(plan[ACTIVE + m : ACTIVE + m + 1, :]) > 0
    after[...] = before[...]

    @pl.when(jnp.logical_not(active))
    def _():
        part_ref[...] = jnp.zeros_like(part_ref)

    @pl.when(active)
    def _():
        acc[...] = jnp.zeros_like(acc)
        row = lax.broadcasted_iota(jnp.int32, (BLK, 1), 0)
        key_pos = jnp.concatenate(
            [row + plan[BASE0 + m : BASE0 + m + 1, 0:1], row + plan[BASE1 + m : BASE1 + m + 1, 0:1]], axis=0
        )

        def step(c, carry):
            at = pl.multiple_of(c * CHUNK, CHUNK)
            cols = pl.ds(at, CHUNK)
            q = q_ref[cols, :]
            do = do_ref[cols, :]
            allowed = (key_pos >= span[0:1, cols]) & (key_pos <= span[1:2, cols])
            s = lax.dot_general(kv[:, :dh], q, NT, preferred_element_type=jnp.float32)
            p = jnp.where(allowed, jnp.exp2(s * (scale * LOG2E) - stats[0:1, cols]), 0.0)
            dp = lax.dot_general(kv[:, dh:], do, NT, preferred_element_type=jnp.float32)
            ds = (p * (dp - stats[1:2, cols])).astype(jnp.bfloat16)
            acc[:, dh:] += jnp.dot(p.astype(jnp.bfloat16), do, preferred_element_type=jnp.float32)
            acc[:, :dh] += jnp.dot(ds, q, preferred_element_type=jnp.float32)
            ds_ref[:, cols] = ds
            return carry

        lax.fori_loop(0, rows // CHUNK, step, 0)
        part_ref[:, :dh] = (acc[:, :dh] * scale).astype(part_ref.dtype)
        part_ref[:, dh:] = acc[:, dh:].astype(part_ref.dtype)


def query_kernel(plan, kv0, kv1, kv2, kv3, ds0, ds1, ds2, ds3, before, dq_ref, after, acc):
    rows, dh = dq_ref.shape
    after[...] = before[...]
    acc[...] = jnp.zeros_like(acc)
    for m, (kv, ds) in enumerate(((kv0, ds0), (kv1, ds1), (kv2, ds2), (kv3, ds3))):

        @pl.when(jnp.max(plan[ACTIVE + m : ACTIVE + m + 1, :]) > 0)
        def _():
            def step(c, carry):
                cols = pl.ds(pl.multiple_of(c * CHUNK, CHUNK), CHUNK)
                acc[:, cols] += lax.dot_general(
                    kv[:, :dh], ds[:, cols], TN, preferred_element_type=jnp.float32
                )
                return carry

            lax.fori_loop(0, rows // CHUNK, step, 0)

    def finish(c, carry):
        cols = pl.ds(pl.multiple_of(c * CHUNK, CHUNK), CHUNK)
        dq_ref[cols, :] = (acc[:, cols] * dh ** (-0.5)).T.astype(dq_ref.dtype)
        return carry

    lax.fori_loop(0, rows // CHUNK, finish, 0)


def total_kernel(plan, part0, part1, part2, part3, before, keep_ref, send_ref):
    parts = (part0, part1, part2, part3)
    wide = part0.shape[1] // LANES
    wants = [jnp.concatenate([plan[WANT + m : WANT + m + 1, :]] * wide, axis=1) for m in range(4)]
    for z in range(ZL):
        keep = jnp.zeros((BLK, wide * LANES), jnp.float32)
        send = jnp.zeros((BLK, wide * LANES), jnp.float32)
        for m in range(4):
            here = wants[m] == z
            keep += jnp.where(here, parts[m][:BLK, :].astype(jnp.float32), 0.0)
            send += jnp.where(here, parts[m][BLK:, :].astype(jnp.float32), 0.0)
        keep_ref[z] = keep
        send_ref[z] = send.astype(send_ref.dtype)


def finish_kernel(moved, gk_ref, gv_ref):
    dh = moved.shape[2] // 2
    for k in range(KVH):
        grad = moved[k].astype(jnp.float32)
        for z in range(1, ZL):
            grad += moved[z * KVH + k].astype(jnp.float32)
        gk_ref[:, k * dh : (k + 1) * dh] = grad[:, :dh].astype(gk_ref.dtype)
        gv_ref[:, k * dh : (k + 1) * dh] = grad[:, dh:].astype(gv_ref.dtype)


def swap(x, axis, size, mask):
    return lax.ppermute(x, axis, [(i, i ^ mask) for i in range(size)])


def local(queries, keys, values, outputs, out_grad, logsumexp, doc_lengths, block_order):
    rows, heads, dh = queries.shape
    cols = rows * heads
    wide = 2 * dh
    bf16, f32 = jnp.bfloat16, jnp.float32
    shape = jax.ShapeDtypeStruct

    own = jnp.concatenate([keys[:, 0, :], values[:, 0, :]], axis=1)
    column = [own] + [swap(own, "zl", ZL, m) for m in (1, 2, 3)]
    plan, span = call(
        functools.partial(plan_kernel, group=heads),
        (shape((24, LANES), jnp.int32), shape((2, cols), jnp.int32)),
        (block_order, doc_lengths), "plan", specs=[SMEM, SMEM],
    )
    delta = jnp.sum(out_grad.astype(f32) * outputs.astype(f32), axis=2)
    stats = jnp.stack([(logsumexp * LOG2E).T.reshape(-1), delta.reshape(-1)])
    q = queries.reshape(cols, dh)
    do = out_grad.reshape(cols, dh)
    stacked, token = call(
        stack_kernel, (shape((4, BLK, wide), bf16), shape((8, LANES), f32)),
        (*column, plan, span, stats), "stacked",
    )
    theirs = swap(stacked, "core", NCORE, 1)

    pair = shape((2 * BLK, wide), bf16)
    sends = call(select_kernel, (pair,) * 4, (plan, *column, theirs), "select")
    kvs = [sends[0]] + [swap(sends[m], "y", NY, m) for m in (1, 2, 3)]
    parts, dss = [None] * 4, [None] * 4
    for m in (0, 2, 1, 3):
        parts[m], dss[m], token = call(
            functools.partial(class_kernel, m=m),
            (shape((2 * BLK, wide), f32 if m == 0 else bf16), shape((2 * BLK, cols), bf16), shape((8, LANES), f32)),
            (plan, q, do, stats, span, kvs[m], token), "class" + str(m),
            scratch=[pltpu.VMEM((2 * BLK, wide), f32)],
            flops=8 * cols * 2 * BLK * dh, moved=3 * cols * dh * 2,
        )
    back = [parts[0]] + [swap(parts[m], "y", NY, m) for m in (1, 2, 3)]
    grad_q, token = call(
        query_kernel, (shape((cols, dh), bf16), shape((8, LANES), f32)), (plan, *kvs, *dss, token), "query",
        scratch=[pltpu.VMEM((dh, cols), f32)], flops=8 * cols * 2 * BLK * dh, moved=8 * cols * dh * 2,
    )

    keep, send = call(
        total_kernel, (shape((ZL, BLK, wide), f32), shape((ZL, BLK, wide), bf16)), (plan, *back, token), "total"
    )
    mine = call(add_kernel, shape((ZL, BLK, wide), bf16), (keep, swap(send, "core", NCORE, 1)), "add")
    share = BLK // KVH
    moved = lax.all_to_all(
        mine.reshape(ZL * KVH, share, wide), ("zl", "x", "zh"), split_axis=0, concat_axis=0, tiled=True
    )
    out = shape((share, KVH * dh), bf16)
    grad_keys, grad_values = call(finish_kernel, (out, out), (moved,), "finish")
    return grad_q.reshape(rows, heads, dh), grad_keys, grad_values


def solution(mesh):
    fine = Mesh(mesh.devices.reshape(ZL, NY, NCORE, NX, ZH), ("zl", "y", "core", "x", "zh"))
    ctx, kv = ("zl", "y", "core"), ("x", "zh")
    in_specs = (P(ctx, kv, None),) * 5 + (P(kv, ctx), P(), P())
    out_specs = (P(ctx, kv, None), P(ctx + kv, None), P(ctx + kv, None))
    return jax.shard_map(local, mesh=fine, in_specs=in_specs, out_specs=out_specs, check_vma=False)
```

```python
import functools

import jax
import jax.numpy as jnp
from jax import lax
from jax.experimental import pallas as pl
from jax.experimental.pallas import tpu as pltpu
from jax.sharding import Mesh
from jax.sharding import PartitionSpec as P

BLK = 128
WIN = 5
ZL, NY, NCORE, NX, ZH = 4, 4, 2, 4, 2
KVH = NX * ZH
LOG2E = 1.4426950408889634
CHUNK = 1024
ORDER = (0, 2, 1, 3)
LANES = 128
SEND, WANT, BASE = 0, 8, 16
NT = (((1,), (1,)), ((), ()))
TN = (((0,), (0,)), ((), ()))
SMEM = pl.BlockSpec(memory_space=pltpu.SMEM)
VMEM = pl.BlockSpec(memory_space=pltpu.VMEM)


def call(body, outs, inputs, name, scratch=(), specs=None, flops=0, moved=1 << 18):
    return pl.pallas_call(
        body,
        out_shape=outs,
        in_specs=specs or [VMEM] * len(inputs),
        out_specs=jax.tree.map(lambda _: VMEM, outs),
        scratch_shapes=scratch,
        compiler_params=pltpu.CompilerParams(vmem_limit_bytes=16 * 1024 * 1024),
        cost_estimate=pl.CostEstimate(flops=flops, bytes_accessed=moved, transcendentals=0),
        name=name,
    )(*inputs)


def plan_kernel(order, lengths, plan_ref, span_ref, *, group):
    zl, y, core = lax.axis_index("zl"), lax.axis_index("y"), lax.axis_index("core")
    ends, total = [], 0
    for k in range(lengths.shape[0]):
        total = total + lengths[k]
        ends.append(total)

    def put(row, value):
        plan_ref[row : row + 1, :] = jnp.full((1, LANES), value, jnp.int32)

    cols = span_ref.shape[1]
    for j in range(2):
        me = order[(zl * NY + y) * NCORE + (core ^ j)]
        q_first = me * BLK
        mine = jnp.maximum(lax.shift_right_logical(me, 1) - 2, 0)
        for m in range(4):
            near = order[(zl * NY + (y ^ m)) * NCORE + (core ^ j)]
            first = jnp.maximum(lax.shift_right_logical(near, 1) - 2, 0)
            pair = jnp.minimum(first + ((y - first) & 3), 15)
            want = lax.shift_right_logical(pair, 2)
            put(SEND + 2 * m + j, zl ^ want)
            put(WANT + 2 * m + j, want)
            offset = ((y ^ m) - mine) & 3
            low = ((mine + offset) * 2 + core) * BLK
            put(BASE + 2 * m + j, low)
        pos = q_first + lax.broadcasted_iota(jnp.int32, (1, cols), 1) // group
        start = jnp.zeros((1, cols), jnp.int32)
        for end in ends:
            start = jnp.where(end <= pos, end, start)
        span_ref[2 * j : 2 * j + 1, :] = start
        span_ref[2 * j + 1 : 2 * j + 2, :] = pos


def select_kernel(plan, own, col1, col2, col3, *outs):
    column = (own, col1, col2, col3)
    for m in range(4):
        for j in range(2):
            row = SEND + 2 * m + j
            at = jnp.concatenate([plan[row : row + 1, :]] * (own.shape[1] // LANES), axis=1)
            block = own[...]
            for s in range(1, 4):
                block = jnp.where(at == s, column[s][...], block)
            outs[m][j * BLK : (j + 1) * BLK, :] = block


def class_kernel(plan, q0, do0, stats0, q1, do1, stats1, span, kv, before, part_ref, ds_ref, after, *, m):
    rows, dh = q0.shape
    scale = dh ** (-0.5)
    after[...] = before[...]
    sides = ((q0, do0, stats0), (q1, do1, stats1))
    grads = [None, None]
    for c in range(rows // CHUNK):
        cols = slice(c * CHUNK, (c + 1) * CHUNK)
        for j, (q_ref, do_ref, stats) in enumerate(sides):
            keys = slice(j * BLK, (j + 1) * BLK)
            row = BASE + 2 * m + j
            key_pos = lax.broadcasted_iota(jnp.int32, (BLK, 1), 0) + plan[row : row + 1, 0:1]
            allowed = (key_pos >= span[2 * j : 2 * j + 1, cols]) & (key_pos <= span[2 * j + 1 : 2 * j + 2, cols])
            q = q_ref[cols, :]
            do = do_ref[cols, :]
            s = lax.dot_general(kv[keys, :dh], q, NT, preferred_element_type=jnp.float32)
            dp = lax.dot_general(kv[keys, dh:], do, NT, preferred_element_type=jnp.float32)
            p = jnp.where(allowed, jnp.exp2(s * (scale * LOG2E) - stats[0:1, cols]), 0.0)
            ds = (p * (dp - stats[1:2, cols])).astype(jnp.bfloat16)
            ds_ref[keys, cols] = ds
            dv = jnp.dot(p.astype(jnp.bfloat16), do, preferred_element_type=jnp.float32)
            dk = jnp.dot(ds, q, preferred_element_type=jnp.float32)
            grads[j] = (dk, dv) if c == 0 else (grads[j][0] + dk, grads[j][1] + dv)
    for j, (dk, dv) in enumerate(grads):
        keys = slice(j * BLK, (j + 1) * BLK)
        part_ref[keys, :dh] = (dk * scale).astype(part_ref.dtype)
        part_ref[keys, dh:] = dv.astype(part_ref.dtype)


def query_kernel(kv0, kv1, kv2, kv3, ds0, ds1, ds2, ds3, before, mine, theirs, after, kt):
    rows, dh = mine.shape
    after[...] = before[...]
    for j, out in enumerate((mine, theirs)):
        keys = slice(j * BLK, (j + 1) * BLK)
        for m, kv in enumerate((kv0, kv1, kv2, kv3)):
            kt[:, m * BLK : (m + 1) * BLK] = kv[keys, :dh].T

        def step(c, carry):
            cols = pl.ds(pl.multiple_of(c * CHUNK, CHUNK), CHUNK)
            ds = jnp.concatenate([ref[keys, cols] for ref in (ds0, ds1, ds2, ds3)], axis=0)
            dq = jnp.dot(kt[...], ds, preferred_element_type=jnp.float32)
            out[cols, :] = (dq * dh ** (-0.5)).T.astype(out.dtype)
            return carry

        lax.fori_loop(0, rows // CHUNK, step, 0)


def join_kernel(mine, theirs, out):
    out[...] = (mine[...] + theirs[...].astype(jnp.float32)).astype(out.dtype)


def total_kernel(plan, part0, part1, part2, part3, before, out, acc):
    acc[...] = jnp.zeros_like(acc)
    for m, part in enumerate((part0, part1, part2, part3)):
        for j in range(2):
            row = WANT + 2 * m + j
            z = jnp.max(plan[row : row + 1, :])
            acc[z] += part[j * BLK : (j + 1) * BLK, :].astype(jnp.float32)
    out[...] = acc[...].astype(out.dtype)


def finish_kernel(moved, gk_ref, gv_ref):
    dh = moved.shape[2] // 2
    for k in range(KVH):
        grad = moved[k].astype(jnp.float32)
        for z in range(1, ZL):
            grad += moved[z * KVH + k].astype(jnp.float32)
        gk_ref[:, k * dh : (k + 1) * dh] = grad[:, :dh].astype(gk_ref.dtype)
        gv_ref[:, k * dh : (k + 1) * dh] = grad[:, dh:].astype(gv_ref.dtype)


def swap(x, axis, size, mask):
    return lax.ppermute(x, axis, [(i, i ^ mask) for i in range(size)])


def local(queries, keys, values, outputs, out_grad, logsumexp, doc_lengths, block_order):
    rows, heads, dh = queries.shape
    cols = rows * heads
    wide = 2 * dh
    bf16, f32 = jnp.bfloat16, jnp.float32
    shape = jax.ShapeDtypeStruct

    own = jnp.concatenate([keys[:, 0, :], values[:, 0, :]], axis=1)
    column = [own] + [swap(own, "zl", ZL, m) for m in (1, 2, 3)]
    plan, span = call(
        functools.partial(plan_kernel, group=heads),
        (shape((24, LANES), jnp.int32), shape((4, cols), jnp.int32)),
        (block_order, doc_lengths), "plan", specs=[SMEM, SMEM],
    )
    delta = jnp.sum(out_grad.astype(f32) * outputs.astype(f32), axis=2)
    stats = jnp.stack([(logsumexp * LOG2E).T.reshape(-1), delta.reshape(-1)])
    sides = []
    for x in (queries.reshape(cols, dh), out_grad.reshape(cols, dh), stats):
        sides.append((x, swap(x, "core", NCORE, 1)))
    near, far = zip(*sides)

    pair = shape((2 * BLK, wide), bf16)
    sends = call(select_kernel, (pair,) * 4, (plan, *column), "select")
    kvs = [sends[0]] + [swap(sends[m], "y", NY, m) for m in (1, 2, 3)]
    token = jnp.zeros((8, LANES), f32)
    parts, dss = [None] * 4, [None] * 4
    for m in ORDER:
        parts[m], dss[m], token = call(
            functools.partial(class_kernel, m=m),
            (shape((2 * BLK, wide), f32 if m == 0 else bf16), shape((2 * BLK, cols), bf16), shape((8, LANES), f32)),
            (plan, *near, *far, span, kvs[m], token), "class" + str(m),
            flops=0, moved=1 << 12,
        )
    back = [parts[0]] + [swap(parts[m], "y", NY, m) for m in (1, 2, 3)]
    mine, theirs, token = call(
        query_kernel, (shape((cols, dh), f32), shape((cols, dh), bf16), shape((8, LANES), f32)),
        (*kvs, *dss, token), "query", scratch=[pltpu.VMEM((dh, 4 * BLK), bf16)],
        flops=0, moved=1<<12,
    )
    grad_q = call(join_kernel, shape((cols, dh), bf16), (mine, swap(theirs, "core", NCORE, 1)), "join", moved=1 << 21)

    total = call(
        total_kernel, shape((ZL, BLK, wide), bf16), (plan, *back, token), "total",
        scratch=[pltpu.VMEM((ZL, BLK, wide), f32)],
    )
    share = BLK // KVH
    moved = lax.all_to_all(
        total.reshape(ZL * KVH, share, wide), ("zl", "x", "zh"), split_axis=0, concat_axis=0, tiled=True
    )
    out = shape((share, KVH * dh), bf16)
    grad_keys, grad_values = call(finish_kernel, (out, out), (moved,), "finish")
    return grad_q.reshape(rows, heads, dh), grad_keys, grad_values


def solution(mesh):
    fine = Mesh(mesh.devices.reshape(ZL, NY, NCORE, NX, ZH), ("zl", "y", "core", "x", "zh"))
    ctx, kv = ("zl", "y", "core"), ("x", "zh")
    in_specs = (P(ctx, kv, None),) * 5 + (P(kv, ctx), P(), P())
    out_specs = (P(ctx, kv, None), P(ctx + kv, None), P(ctx + kv, None))
    return jax.shard_map(local, mesh=fine, in_specs=in_specs, out_specs=out_specs, check_vma=False)
```

```python
import functools

import jax
import jax.numpy as jnp
from jax import lax
from jax.experimental import pallas as pl
from jax.experimental.pallas import tpu as pltpu
from jax.sharding import Mesh
from jax.sharding import PartitionSpec as P

BLK = 128
WIN = 5
ZL, NY, NCORE, NX, ZH = 4, 4, 2, 4, 2
KVH = NX * ZH
LOG2E = 1.4426950408889634
CHUNK = 1024
ORDER = (0, 2, 1, 3)
LANES = 128
SEND, WANT, BASE = 0, 8, 16
NT = (((1,), (1,)), ((), ()))
TN = (((0,), (0,)), ((), ()))
SMEM = pl.BlockSpec(memory_space=pltpu.SMEM)
VMEM = pl.BlockSpec(memory_space=pltpu.VMEM)


def call(body, outs, inputs, name, scratch=(), specs=None, flops=0, moved=1 << 18):
    return pl.pallas_call(
        body,
        out_shape=outs,
        in_specs=specs or [VMEM] * len(inputs),
        out_specs=jax.tree.map(lambda _: VMEM, outs),
        scratch_shapes=scratch,
        compiler_params=pltpu.CompilerParams(vmem_limit_bytes=16 * 1024 * 1024),
        cost_estimate=pl.CostEstimate(flops=flops, bytes_accessed=moved, transcendentals=0),
        name=name,
    )(*inputs)


def plan_kernel(order, lengths, plan_ref, span_ref, *, group):
    zl, y, core = lax.axis_index("zl"), lax.axis_index("y"), lax.axis_index("core")
    ends, total = [], 0
    for k in range(lengths.shape[0]):
        total = total + lengths[k]
        ends.append(total)

    def put(row, value):
        plan_ref[row : row + 1, :] = jnp.full((1, LANES), value, jnp.int32)

    cols = span_ref.shape[1]
    for j in range(2):
        me = order[(zl * NY + y) * NCORE + (core ^ j)]
        q_first = me * BLK
        mine = jnp.maximum(lax.shift_right_logical(me, 1) - 2, 0)
        for m in range(4):
            near = order[(zl * NY + (y ^ m)) * NCORE + (core ^ j)]
            first = jnp.maximum(lax.shift_right_logical(near, 1) - 2, 0)
            pair = jnp.minimum(first + ((y - first) & 3), 15)
            want = lax.shift_right_logical(pair, 2)
            put(SEND + 2 * m + j, zl ^ want)
            put(WANT + 2 * m + j, want)
            offset = ((y ^ m) - mine) & 3
            low = ((mine + offset) * 2 + core) * BLK
            put(BASE + 2 * m + j, low)
        pos = q_first + lax.broadcasted_iota(jnp.int32, (1, cols), 1) // group
        start = jnp.zeros((1, cols), jnp.int32)
        for end in ends:
            start = jnp.where(end <= pos, end, start)
        span_ref[2 * j : 2 * j + 1, :] = start
        span_ref[2 * j + 1 : 2 * j + 2, :] = pos


def stats_kernel(outputs, out_grad, lse, stats):
    rows, dh = outputs.shape
    ones = jnp.ones((8, dh), jnp.bfloat16)
    stats[0:1, :] = lse[...]
    for c in range(rows // CHUNK):
        cols = slice(c * CHUNK, (c + 1) * CHUNK)
        product = outputs[cols, :].astype(jnp.float32) * out_grad[cols, :].astype(jnp.float32)
        high = product.astype(jnp.bfloat16)
        low = (product - high.astype(jnp.float32)).astype(jnp.bfloat16)
        delta = lax.dot_general(ones, high, NT, preferred_element_type=jnp.float32)
        delta += lax.dot_general(ones, low, NT, preferred_element_type=jnp.float32)
        stats[1:2, cols] = delta[0:1, :]


def select_kernel(plan, own, col1, col2, col3, *outs):
    column = (own, col1, col2, col3)
    for m in range(4):
        for j in range(2):
            row = SEND + 2 * m + j
            at = jnp.concatenate([plan[row : row + 1, :]] * (own.shape[1] // LANES), axis=1)
            block = own[...]
            for s in range(1, 4):
                block = jnp.where(at == s, column[s][...], block)
            outs[m][j * BLK : (j + 1) * BLK, :] = block


def class_kernel(plan, q0, do0, stats0, q1, do1, stats1, span, kv, before, part_ref, ds_ref, after, *, m):
    rows, dh = q0.shape
    scale = dh ** (-0.5)
    after[...] = before[...]
    sides = ((q0, do0, stats0), (q1, do1, stats1))
    grads = [None, None]
    for c in range(rows // CHUNK):
        cols = slice(c * CHUNK, (c + 1) * CHUNK)
        for j, (q_ref, do_ref, stats) in enumerate(sides):
            keys = slice(j * BLK, (j + 1) * BLK)
            row = BASE + 2 * m + j
            key_pos = lax.broadcasted_iota(jnp.int32, (BLK, 1), 0) + plan[row : row + 1, 0:1]
            allowed = (key_pos >= span[2 * j : 2 * j + 1, cols]) & (key_pos <= span[2 * j + 1 : 2 * j + 2, cols])
            q = q_ref[cols, :]
            do = do_ref[cols, :]
            s = lax.dot_general(kv[keys, :dh], q, NT, preferred_element_type=jnp.float32)
            dp = lax.dot_general(kv[keys, dh:], do, NT, preferred_element_type=jnp.float32)
            p = jnp.where(allowed, jnp.exp2(s * (scale * LOG2E) - stats[0:1, cols]), 0.0)
            ds = (p * (dp - stats[1:2, cols])).astype(jnp.bfloat16)
            ds_ref[keys, cols] = ds
            dv = jnp.dot(p.astype(jnp.bfloat16), do, preferred_element_type=jnp.float32)
            dk = jnp.dot(ds, q, preferred_element_type=jnp.float32)
            grads[j] = (dk, dv) if c == 0 else (grads[j][0] + dk, grads[j][1] + dv)
    for j, (dk, dv) in enumerate(grads):
        keys = slice(j * BLK, (j + 1) * BLK)
        part_ref[keys, :dh] = (dk * scale).astype(part_ref.dtype)
        part_ref[keys, dh:] = dv.astype(part_ref.dtype)


def query_kernel(kv0, kv1, kv2, kv3, ds0, ds1, ds2, ds3, before, mine, theirs, after, kt):
    rows, dh = mine.shape
    after[...] = before[...]
    for j, out in enumerate((mine, theirs)):
        keys = slice(j * BLK, (j + 1) * BLK)
        for m, kv in enumerate((kv0, kv1, kv2, kv3)):
            kt[:, m * BLK : (m + 1) * BLK] = kv[keys, :dh].T

        def step(c, carry):
            cols = pl.ds(pl.multiple_of(c * CHUNK, CHUNK), CHUNK)
            ds = jnp.concatenate([ref[keys, cols] for ref in (ds0, ds1, ds2, ds3)], axis=0)
            dq = jnp.dot(kt[...], ds, preferred_element_type=jnp.float32)
            out[cols, :] = (dq * dh ** (-0.5)).T.astype(out.dtype)
            return carry

        lax.fori_loop(0, rows // CHUNK, step, 0)


def join_kernel(mine, theirs, out):
    out[...] = (mine[...] + theirs[...].astype(jnp.float32)).astype(out.dtype)


def total_kernel(plan, part0, part1, part2, part3, before, out, acc):
    acc[...] = jnp.zeros_like(acc)
    for m, part in enumerate((part0, part1, part2, part3)):
        for j in range(2):
            row = WANT + 2 * m + j
            z = jnp.max(plan[row : row + 1, :])
            acc[z] += part[j * BLK : (j + 1) * BLK, :].astype(jnp.float32)
    for z in range(ZL):
        out[:, z] = acc[z].reshape(KVH, BLK // KVH, acc.shape[2]).astype(out.dtype)


def finish_kernel(moved, gk_ref, gv_ref):
    dh = moved.shape[2] // 2
    for k in range(KVH):
        grad = moved[k * ZL].astype(jnp.float32)
        for z in range(1, ZL):
            grad += moved[k * ZL + z].astype(jnp.float32)
        gk_ref[:, k * dh : (k + 1) * dh] = grad[:, :dh].astype(gk_ref.dtype)
        gv_ref[:, k * dh : (k + 1) * dh] = grad[:, dh:].astype(gv_ref.dtype)


def swap(x, axis, size, mask):
    return lax.ppermute(x, axis, [(i, i ^ mask) for i in range(size)])


def local(queries, keys, values, outputs, out_grad, logsumexp, doc_lengths, block_order):
    rows, heads, dh = queries.shape
    cols = rows * heads
    wide = 2 * dh
    bf16, f32 = jnp.bfloat16, jnp.float32
    shape = jax.ShapeDtypeStruct

    own = jnp.concatenate([keys[:, 0, :], values[:, 0, :]], axis=1)
    column = [own] + [swap(own, "zl", ZL, m) for m in (1, 2, 3)]
    plan, span = call(
        functools.partial(plan_kernel, group=heads),
        (shape((24, LANES), jnp.int32), shape((4, cols), jnp.int32)),
        (block_order, doc_lengths), "plan", specs=[SMEM, SMEM],
    )
    stats = call(
        stats_kernel, shape((2, cols), f32),
        (outputs.reshape(cols, dh), out_grad.reshape(cols, dh), (logsumexp * LOG2E).T.reshape(1, cols)), "stats",
    )
    sides = []
    for x in (queries.reshape(cols, dh), out_grad.reshape(cols, dh), stats):
        sides.append((x, swap(x, "core", NCORE, 1)))
    near, far = zip(*sides)

    pair = shape((2 * BLK, wide), bf16)
    sends = call(select_kernel, (pair,) * 4, (plan, *column), "select")
    kvs = [sends[0]] + [swap(sends[m], "y", NY, m) for m in (1, 2, 3)]
    token = jnp.zeros((8, LANES), f32)
    parts, dss = [None] * 4, [None] * 4
    for m in ORDER:
        parts[m], dss[m], token = call(
            functools.partial(class_kernel, m=m),
            (shape((2 * BLK, wide), f32 if m == 0 else bf16), shape((2 * BLK, cols), bf16), shape((8, LANES), f32)),
            (plan, *near, *far, span, kvs[m], token), "class" + str(m),
            flops=0, moved=1 << 12,
        )
    back = [parts[0]] + [swap(parts[m], "y", NY, m) for m in (1, 2, 3)]
    mine, theirs, token = call(
        query_kernel, (shape((cols, dh), f32), shape((cols, dh), bf16), shape((8, LANES), f32)),
        (*kvs, *dss, token), "query", scratch=[pltpu.VMEM((dh, 4 * BLK), bf16)],
        flops=0, moved=1<<12,
    )
    grad_q = call(join_kernel, shape((cols, dh), bf16), (mine, swap(theirs, "core", NCORE, 1)), "join", moved=1 << 21)

    total = call(
        total_kernel, shape((KVH, ZL, BLK // KVH, wide), bf16), (plan, *back, token), "total",
        scratch=[pltpu.VMEM((ZL, BLK, wide), f32)],
    )
    share = BLK // KVH
    moved = lax.all_to_all(
        total.reshape(ZL * KVH, share, wide), ("x", "zh", "zl"), split_axis=0, concat_axis=0, tiled=True
    )
    out = shape((share, KVH * dh), bf16)
    grad_keys, grad_values = call(finish_kernel, (out, out), (moved,), "finish")
    return grad_q.reshape(rows, heads, dh), grad_keys, grad_values


def solution(mesh):
    fine = Mesh(mesh.devices.reshape(ZL, NY, NCORE, NX, ZH), ("zl", "y", "core", "x", "zh"))
    ctx, kv = ("zl", "y", "core"), ("x", "zh")
    in_specs = (P(ctx, kv, None),) * 5 + (P(kv, ctx), P(), P())
    out_specs = (P(ctx, kv, None), P(ctx + kv, None), P(ctx + kv, None))
    return jax.shard_map(local, mesh=fine, in_specs=in_specs, out_specs=out_specs, check_vma=False)
```

```python
import functools

import jax
import jax.numpy as jnp
from jax import lax
from jax.experimental import pallas as pl
from jax.experimental.pallas import tpu as pltpu
from jax.sharding import Mesh
from jax.sharding import PartitionSpec as P

BLK = 128
WIN = 5
ZL, NY, NCORE, NX, ZH = 4, 4, 2, 4, 2
KVH = NX * ZH
LOG2E = 1.4426950408889634
CHUNK = 1024
ORDER = (0, 2, 1, 3)
LANES = 128
SEND, WANT, BASE = 0, 8, 16
NT = (((1,), (1,)), ((), ()))
TN = (((0,), (0,)), ((), ()))
SMEM = pl.BlockSpec(memory_space=pltpu.SMEM)
VMEM = pl.BlockSpec(memory_space=pltpu.VMEM)


def call(body, outs, inputs, name, scratch=(), specs=None, flops=0, moved=1 << 18):
    return pl.pallas_call(
        body,
        out_shape=outs,
        in_specs=specs or [VMEM] * len(inputs),
        out_specs=jax.tree.map(lambda _: VMEM, outs),
        scratch_shapes=scratch,
        compiler_params=pltpu.CompilerParams(vmem_limit_bytes=16 * 1024 * 1024),
        cost_estimate=pl.CostEstimate(flops=flops, bytes_accessed=moved, transcendentals=0),
        name=name,
    )(*inputs)


def plan_kernel(order, lengths, plan_ref, span_ref, *, group):
    zl, y, core = lax.axis_index("zl"), lax.axis_index("y"), lax.axis_index("core")
    ends, total = [], 0
    for k in range(lengths.shape[0]):
        total = total + lengths[k]
        ends.append(total)

    def put(row, value):
        plan_ref[row : row + 1, :] = jnp.full((1, LANES), value, jnp.int32)

    cols = span_ref.shape[1]
    for j in range(2):
        me = order[(zl * NY + y) * NCORE + (core ^ j)]
        q_first = me * BLK
        mine = jnp.maximum(lax.shift_right_logical(me, 1) - 2, 0)
        for m in range(4):
            near = order[(zl * NY + (y ^ m)) * NCORE + (core ^ j)]
            first = jnp.maximum(lax.shift_right_logical(near, 1) - 2, 0)
            pair = jnp.minimum(first + ((y - first) & 3), 15)
            want = lax.shift_right_logical(pair, 2)
            put(SEND + 2 * m + j, zl ^ want)
            put(WANT + 2 * m + j, want)
            offset = ((y ^ m) - mine) & 3
            low = ((mine + offset) * 2 + core) * BLK
            put(BASE + 2 * m + j, low)
        pos = q_first + lax.broadcasted_iota(jnp.int32, (1, cols), 1) // group
        start = jnp.zeros((1, cols), jnp.int32)
        for end in ends:
            start = jnp.where(end <= pos, end, start)
        span_ref[2 * j : 2 * j + 1, :] = start
        span_ref[2 * j + 1 : 2 * j + 2, :] = pos


def stats_kernel(outputs, out_grad, lse, stats, loaded, sems):
    rows, dh = outputs.shape
    copies = []
    for c in range(rows // CHUNK):
        cols = pl.ds(c * CHUNK, CHUNK)
        for i, ref in enumerate((outputs, out_grad)):
            copy = pltpu.make_async_copy(ref.at[cols, :], loaded.at[i, cols, :], sems.at[c, i])
            copy.start()
            copies.append(copy)
    ones = jnp.ones((8, dh), jnp.bfloat16)
    stats[0:1, :] = lse[...]
    for c in range(rows // CHUNK):
        cols = slice(c * CHUNK, (c + 1) * CHUNK)
        copies[2 * c].wait()
        copies[2 * c + 1].wait()
        product = loaded[0, cols, :].astype(jnp.float32) * loaded[1, cols, :].astype(jnp.float32)
        high = product.astype(jnp.bfloat16)
        low = (product - high.astype(jnp.float32)).astype(jnp.bfloat16)
        delta = lax.dot_general(ones, high, NT, preferred_element_type=jnp.float32)
        delta += lax.dot_general(ones, low, NT, preferred_element_type=jnp.float32)
        stats[1:2, cols] = delta[0:1, :]


def select_kernel(plan, own, col1, col2, col3, *outs):
    column = (own, col1, col2, col3)
    for m in range(4):
        for j in range(2):
            row = SEND + 2 * m + j
            at = jnp.concatenate([plan[row : row + 1, :]] * (own.shape[1] // LANES), axis=1)
            block = own[...]
            for s in range(1, 4):
                block = jnp.where(at == s, column[s][...], block)
            outs[m][j * BLK : (j + 1) * BLK, :] = block


def class_kernel(plan, q0, do0, stats0, q1, do1, stats1, span, kv, before, part_ref, ds_ref, after, *, m):
    rows, dh = q0.shape
    scale = dh ** (-0.5)
    after[...] = before[...]
    sides = ((q0, do0, stats0), (q1, do1, stats1))
    grads = [None, None]
    for c in range(rows // CHUNK):
        cols = slice(c * CHUNK, (c + 1) * CHUNK)
        for j, (q_ref, do_ref, stats) in enumerate(sides):
            keys = slice(j * BLK, (j + 1) * BLK)
            row = BASE + 2 * m + j
            key_pos = lax.broadcasted_iota(jnp.int32, (BLK, 1), 0) + plan[row : row + 1, 0:1]
            allowed = (key_pos >= span[2 * j : 2 * j + 1, cols]) & (key_pos <= span[2 * j + 1 : 2 * j + 2, cols])
            q = q_ref[cols, :]
            do = do_ref[cols, :]
            s = lax.dot_general(kv[keys, :dh], q, NT, preferred_element_type=jnp.float32)
            dp = lax.dot_general(kv[keys, dh:], do, NT, preferred_element_type=jnp.float32)
            p = jnp.where(allowed, jnp.exp2(s * (scale * LOG2E) - stats[0:1, cols]), 0.0)
            ds = (p * (dp - stats[1:2, cols])).astype(jnp.bfloat16)
            ds_ref[keys, cols] = ds
            dv = jnp.dot(p.astype(jnp.bfloat16), do, preferred_element_type=jnp.float32)
            dk = jnp.dot(ds, q, preferred_element_type=jnp.float32)
            grads[j] = (dk, dv) if c == 0 else (grads[j][0] + dk, grads[j][1] + dv)
    for j, (dk, dv) in enumerate(grads):
        keys = slice(j * BLK, (j + 1) * BLK)
        part_ref[keys, :dh] = (dk * scale).astype(part_ref.dtype)
        part_ref[keys, dh:] = dv.astype(part_ref.dtype)


def query_kernel(kv0, kv1, kv2, kv3, ds0, ds1, ds2, ds3, before, mine, theirs, after, kt):
    rows, dh = mine.shape
    after[...] = before[...]
    for j, out in enumerate((mine, theirs)):
        keys = slice(j * BLK, (j + 1) * BLK)
        for m, kv in enumerate((kv0, kv1, kv2, kv3)):
            kt[:, m * BLK : (m + 1) * BLK] = kv[keys, :dh].T

        def step(c, carry):
            cols = pl.ds(pl.multiple_of(c * CHUNK, CHUNK), CHUNK)
            ds = jnp.concatenate([ref[keys, cols] for ref in (ds0, ds1, ds2, ds3)], axis=0)
            dq = jnp.dot(kt[...], ds, preferred_element_type=jnp.float32)
            out[cols, :] = (dq * dh ** (-0.5)).T.astype(out.dtype)
            return carry

        lax.fori_loop(0, rows // CHUNK, step, 0)


def join_kernel(mine, theirs, out):
    out[...] = (mine[...] + theirs[...].astype(jnp.float32)).astype(out.dtype)


def total_kernel(plan, part0, part1, part2, part3, before, out, acc):
    acc[...] = jnp.zeros_like(acc)
    for m, part in enumerate((part0, part1, part2, part3)):
        for j in range(2):
            row = WANT + 2 * m + j
            z = jnp.max(plan[row : row + 1, :])
            acc[z] += part[j * BLK : (j + 1) * BLK, :].astype(jnp.float32)
    for z in range(ZL):
        out[:, z] = acc[z].reshape(KVH, BLK // KVH, acc.shape[2]).astype(out.dtype)


def finish_kernel(moved, gk_ref, gv_ref):
    dh = moved.shape[2] // 2
    for k in range(KVH):
        grad = moved[k * ZL].astype(jnp.float32)
        for z in range(1, ZL):
            grad += moved[k * ZL + z].astype(jnp.float32)
        gk_ref[:, k * dh : (k + 1) * dh] = grad[:, :dh].astype(gk_ref.dtype)
        gv_ref[:, k * dh : (k + 1) * dh] = grad[:, dh:].astype(gv_ref.dtype)


def swap(x, axis, size, mask):
    return lax.ppermute(x, axis, [(i, i ^ mask) for i in range(size)])


def local(queries, keys, values, outputs, out_grad, logsumexp, doc_lengths, block_order):
    rows, heads, dh = queries.shape
    cols = rows * heads
    wide = 2 * dh
    bf16, f32 = jnp.bfloat16, jnp.float32
    shape = jax.ShapeDtypeStruct

    own = jnp.concatenate([keys[:, 0, :], values[:, 0, :]], axis=1)
    column = [own] + [swap(own, "zl", ZL, m) for m in (1, 2, 3)]
    plan, span = call(
        functools.partial(plan_kernel, group=heads),
        (shape((24, LANES), jnp.int32), shape((4, cols), jnp.int32)),
        (block_order, doc_lengths), "plan", specs=[SMEM, SMEM],
    )
    stats = call(
        stats_kernel, shape((2, cols), f32),
        (outputs.reshape(cols, dh), out_grad.reshape(cols, dh), (logsumexp * LOG2E).T.reshape(1, cols)), "stats",
        scratch=[pltpu.VMEM((2, cols, dh), bf16), pltpu.SemaphoreType.DMA((cols // CHUNK, 2))],
        specs=[pl.BlockSpec(memory_space=pl.ANY)] * 2 + [VMEM], moved=1 << 22,
    )
    sides = []
    for x in (queries.reshape(cols, dh), out_grad.reshape(cols, dh), stats):
        sides.append((x, swap(x, "core", NCORE, 1)))
    near, far = zip(*sides)

    pair = shape((2 * BLK, wide), bf16)
    sends = call(select_kernel, (pair,) * 4, (plan, *column), "select")
    kvs = [sends[0]] + [swap(sends[m], "y", NY, m) for m in (1, 2, 3)]
    token = jnp.zeros((8, LANES), f32)
    parts, dss = [None] * 4, [None] * 4
    for m in ORDER:
        parts[m], dss[m], token = call(
            functools.partial(class_kernel, m=m),
            (shape((2 * BLK, wide), f32 if m == 0 else bf16), shape((2 * BLK, cols), bf16), shape((8, LANES), f32)),
            (plan, *near, *far, span, kvs[m], token), "class" + str(m),
            flops=0, moved=1 << 12,
        )
    back = [parts[0]] + [swap(parts[m], "y", NY, m) for m in (1, 2, 3)]
    mine, theirs, token = call(
        query_kernel, (shape((cols, dh), f32), shape((cols, dh), bf16), shape((8, LANES), f32)),
        (*kvs, *dss, token), "query", scratch=[pltpu.VMEM((dh, 4 * BLK), bf16)],
        flops=0, moved=1<<12,
    )
    grad_q = call(join_kernel, shape((cols, dh), bf16), (mine, swap(theirs, "core", NCORE, 1)), "join", moved=1 << 21)

    total = call(
        total_kernel, shape((KVH, ZL, BLK // KVH, wide), bf16), (plan, *back, token), "total",
        scratch=[pltpu.VMEM((ZL, BLK, wide), f32)],
    )
    share = BLK // KVH
    moved = lax.all_to_all(
        total.reshape(ZL * KVH, share, wide), ("x", "zh", "zl"), split_axis=0, concat_axis=0, tiled=True
    )
    out = shape((share, KVH * dh), bf16)
    grad_keys, grad_values = call(finish_kernel, (out, out), (moved,), "finish")
    return grad_q.reshape(rows, heads, dh), grad_keys, grad_values


def solution(mesh):
    fine = Mesh(mesh.devices.reshape(ZL, NY, NCORE, NX, ZH), ("zl", "y", "core", "x", "zh"))
    ctx, kv = ("zl", "y", "core"), ("x", "zh")
    in_specs = (P(ctx, kv, None),) * 5 + (P(kv, ctx), P(), P())
    out_specs = (P(ctx, kv, None), P(ctx + kv, None), P(ctx + kv, None))
    return jax.shard_map(local, mesh=fine, in_specs=in_specs, out_specs=out_specs, check_vma=False)
```

```python
import functools

import jax
import jax.numpy as jnp
from jax import lax
from jax.experimental import pallas as pl
from jax.experimental.pallas import tpu as pltpu
from jax.sharding import Mesh
from jax.sharding import PartitionSpec as P

BLK = 128
WIN = 5
ZL, NY, NCORE, NX, ZH = 4, 4, 2, 4, 2
KVH = NX * ZH
LOG2E = 1.4426950408889634
CHUNK = 1024
ORDER = (0, 2, 1, 3)
LANES = 128
SEND, WANT, BASE = 0, 8, 16
NT = (((1,), (1,)), ((), ()))
TN = (((0,), (0,)), ((), ()))
SMEM = pl.BlockSpec(memory_space=pltpu.SMEM)
VMEM = pl.BlockSpec(memory_space=pltpu.VMEM)


def call(body, outs, inputs, name, scratch=(), specs=None, flops=0, moved=1 << 18):
    return pl.pallas_call(
        body,
        out_shape=outs,
        in_specs=specs or [VMEM] * len(inputs),
        out_specs=jax.tree.map(lambda _: VMEM, outs),
        scratch_shapes=scratch,
        compiler_params=pltpu.CompilerParams(vmem_limit_bytes=16 * 1024 * 1024),
        cost_estimate=pl.CostEstimate(flops=flops, bytes_accessed=moved, transcendentals=0),
        name=name,
    )(*inputs)


def plan_kernel(order, lengths, plan_ref, span_ref, *, group):
    zl, y, core = lax.axis_index("zl"), lax.axis_index("y"), lax.axis_index("core")
    ends, total = [], 0
    for k in range(lengths.shape[0]):
        total = total + lengths[k]
        ends.append(total)

    def put(row, value):
        plan_ref[row : row + 1, :] = jnp.full((1, LANES), value, jnp.int32)

    cols = span_ref.shape[1]
    for j in range(2):
        me = order[(zl * NY + y) * NCORE + (core ^ j)]
        q_first = me * BLK
        mine = jnp.maximum(lax.shift_right_logical(me, 1) - 2, 0)
        for m in range(4):
            near = order[(zl * NY + (y ^ m)) * NCORE + (core ^ j)]
            first = jnp.maximum(lax.shift_right_logical(near, 1) - 2, 0)
            pair = jnp.minimum(first + ((y - first) & 3), 15)
            want = lax.shift_right_logical(pair, 2)
            put(SEND + 2 * m + j, zl ^ want)
            put(WANT + 2 * m + j, want)
            offset = ((y ^ m) - mine) & 3
            low = ((mine + offset) * 2 + core) * BLK
            put(BASE + 2 * m + j, low)
        pos = q_first + lax.broadcasted_iota(jnp.int32, (1, cols), 1) // group
        start = jnp.zeros((1, cols), jnp.int32)
        for end in ends:
            start = jnp.where(end <= pos, end, start)
        span_ref[2 * j : 2 * j + 1, :] = start
        span_ref[2 * j + 1 : 2 * j + 2, :] = pos


def select_kernel(plan, own, col1, col2, col3, *outs):
    column = (own, col1, col2, col3)
    for m in range(4):
        for j in range(2):
            row = SEND + 2 * m + j
            at = jnp.concatenate([plan[row : row + 1, :]] * (own.shape[1] // LANES), axis=1)
            block = own[...]
            for s in range(1, 4):
                block = jnp.where(at == s, column[s][...], block)
            outs[m][j * BLK : (j + 1) * BLK, :] = block


def class_kernel(plan, q0, do0, stats0, q1, do1, stats1, span, kv, before, part_ref, ds_ref, after, *, m):
    rows, dh = q0.shape
    scale = dh ** (-0.5)
    after[...] = before[...]
    sides = ((q0, do0, stats0), (q1, do1, stats1))
    grads = [None, None]
    for c in range(rows // CHUNK):
        cols = slice(c * CHUNK, (c + 1) * CHUNK)
        for j, (q_ref, do_ref, stats) in enumerate(sides):
            keys = slice(j * BLK, (j + 1) * BLK)
            row = BASE + 2 * m + j
            key_pos = lax.broadcasted_iota(jnp.int32, (BLK, 1), 0) + plan[row : row + 1, 0:1]
            allowed = (key_pos >= span[2 * j : 2 * j + 1, cols]) & (key_pos <= span[2 * j + 1 : 2 * j + 2, cols])
            q = q_ref[cols, :]
            do = do_ref[cols, :]
            s = lax.dot_general(kv[keys, :dh], q, NT, preferred_element_type=jnp.float32)
            dp = lax.dot_general(kv[keys, dh:], do, NT, preferred_element_type=jnp.float32)
            p = jnp.where(allowed, jnp.exp2(s * (scale * LOG2E) - stats[0:1, cols]), 0.0)
            ds = (p * (dp - stats[1:2, cols])).astype(jnp.bfloat16)
            ds_ref[keys, cols] = ds
            dv = jnp.dot(p.astype(jnp.bfloat16), do, preferred_element_type=jnp.float32)
            dk = jnp.dot(ds, q, preferred_element_type=jnp.float32)
            grads[j] = (dk, dv) if c == 0 else (grads[j][0] + dk, grads[j][1] + dv)
    for j, (dk, dv) in enumerate(grads):
        keys = slice(j * BLK, (j + 1) * BLK)
        part_ref[keys, :dh] = (dk * scale).astype(part_ref.dtype)
        part_ref[keys, dh:] = dv.astype(part_ref.dtype)


def query_kernel(kv0, kv1, kv2, kv3, ds0, ds1, ds2, ds3, before, mine, theirs, after, kt):
    rows, dh = mine.shape
    after[...] = before[...]
    for j, out in enumerate((mine, theirs)):
        keys = slice(j * BLK, (j + 1) * BLK)
        for m, kv in enumerate((kv0, kv1, kv2, kv3)):
            kt[:, m * BLK : (m + 1) * BLK] = kv[keys, :dh].T

        def step(c, carry):
            cols = pl.ds(pl.multiple_of(c * CHUNK, CHUNK), CHUNK)
            ds = jnp.concatenate([ref[keys, cols] for ref in (ds0, ds1, ds2, ds3)], axis=0)
            dq = jnp.dot(kt[...], ds, preferred_element_type=jnp.float32)
            out[cols, :] = (dq * dh ** (-0.5)).T.astype(out.dtype)
            return carry

        lax.fori_loop(0, rows // CHUNK, step, 0)


def join_kernel(mine, theirs, out):
    out[...] = (mine[...] + theirs[...].astype(jnp.float32)).astype(out.dtype)


def total_kernel(plan, part0, part1, part2, part3, before, out, acc):
    acc[...] = jnp.zeros_like(acc)
    for m, part in enumerate((part0, part1, part2, part3)):
        for j in range(2):
            row = WANT + 2 * m + j
            z = jnp.max(plan[row : row + 1, :])
            acc[z] += part[j * BLK : (j + 1) * BLK, :].astype(jnp.float32)
    for z in range(ZL):
        out[:, z] = acc[z].reshape(KVH, BLK // KVH, acc.shape[2]).astype(out.dtype)


def finish_kernel(moved, gk_ref, gv_ref):
    dh = moved.shape[2] // 2
    for k in range(KVH):
        grad = moved[k * ZL].astype(jnp.float32)
        for z in range(1, ZL):
            grad += moved[k * ZL + z].astype(jnp.float32)
        gk_ref[:, k * dh : (k + 1) * dh] = grad[:, :dh].astype(gk_ref.dtype)
        gv_ref[:, k * dh : (k + 1) * dh] = grad[:, dh:].astype(gv_ref.dtype)


def swap(x, axis, size, mask):
    return lax.ppermute(x, axis, [(i, i ^ mask) for i in range(size)])


def local(queries, keys, values, outputs, out_grad, logsumexp, doc_lengths, block_order):
    rows, heads, dh = queries.shape
    cols = rows * heads
    wide = 2 * dh
    bf16, f32 = jnp.bfloat16, jnp.float32
    shape = jax.ShapeDtypeStruct

    own = jnp.concatenate([keys[:, 0, :], values[:, 0, :]], axis=1)
    column = [own] + [swap(own, "zl", ZL, m) for m in (1, 2, 3)]
    plan, span = call(
        functools.partial(plan_kernel, group=heads),
        (shape((24, LANES), jnp.int32), shape((4, cols), jnp.int32)),
        (block_order, doc_lengths), "plan", specs=[SMEM, SMEM],
    )
    delta = jnp.sum(out_grad.astype(f32) * outputs.astype(f32), axis=2)
    stats = jnp.stack([(logsumexp * LOG2E).T.reshape(-1), delta.reshape(-1)])
    sides = []
    for x in (queries.reshape(cols, dh), out_grad.reshape(cols, dh), stats):
        sides.append((x, swap(x, "core", NCORE, 1)))
    near, far = zip(*sides)

    pair = shape((2 * BLK, wide), bf16)
    sends = call(select_kernel, (pair,) * 4, (plan, *column), "select")
    kvs = [sends[0]] + [swap(sends[m], "y", NY, m) for m in (1, 2, 3)]
    token = jnp.zeros((8, LANES), f32)
    parts, dss = [None] * 4, [None] * 4
    for m in ORDER:
        parts[m], dss[m], token = call(
            functools.partial(class_kernel, m=m),
            (shape((2 * BLK, wide), f32 if m == 0 else bf16), shape((2 * BLK, cols), bf16), shape((8, LANES), f32)),
            (plan, *near, *far, span, kvs[m], token), "class" + str(m),
            flops=0, moved=1 << 12,
        )
    back = [parts[0]] + [swap(parts[m], "y", NY, m) for m in (1, 2, 3)]
    mine, theirs, token = call(
        query_kernel, (shape((cols, dh), f32), shape((cols, dh), bf16), shape((8, LANES), f32)),
        (*kvs, *dss, token), "query", scratch=[pltpu.VMEM((dh, 4 * BLK), bf16)],
        flops=0, moved=1<<12,
    )
    grad_q = call(join_kernel, shape((cols, dh), bf16), (mine, swap(theirs, "core", NCORE, 1)), "join", moved=1 << 21)

    total = call(
        total_kernel, shape((KVH, ZL, BLK // KVH, wide), bf16), (plan, *back, token), "total",
        scratch=[pltpu.VMEM((ZL, BLK, wide), f32)],
    )
    share = BLK // KVH
    moved = lax.all_to_all(
        total.reshape(ZL * KVH, share, wide), ("x", "zh", "zl"), split_axis=0, concat_axis=0, tiled=True
    )
    out = shape((share, KVH * dh), bf16)
    grad_keys, grad_values = call(finish_kernel, (out, out), (moved,), "finish")
    return grad_q.reshape(rows, heads, dh), grad_keys, grad_values


def solution(mesh):
    fine = Mesh(mesh.devices.reshape(ZL, NY, NCORE, NX, ZH), ("zl", "y", "core", "x", "zh"))
    ctx, kv = ("zl", "y", "core"), ("x", "zh")
    in_specs = (P(ctx, kv, None),) * 5 + (P(kv, ctx), P(), P())
    out_specs = (P(ctx, kv, None), P(ctx + kv, None), P(ctx + kv, None))
    return jax.shard_map(local, mesh=fine, in_specs=in_specs, out_specs=out_specs, check_vma=False)
```

```python
import functools

import jax
import jax.numpy as jnp
from jax import lax
from jax.experimental import pallas as pl
from jax.experimental.pallas import tpu as pltpu
from jax.sharding import Mesh
from jax.sharding import PartitionSpec as P

BLK = 128
WIN = 5
ZL, NY, NCORE, NX, ZH = 4, 4, 2, 4, 2
KVH = NX * ZH
LOG2E = 1.4426950408889634
CHUNK = 1024
ORDER = (0, 2, 1, 3)
LANES = 128
SEND, WANT, BASE = 0, 8, 16
NT = (((1,), (1,)), ((), ()))
TN = (((0,), (0,)), ((), ()))
SMEM = pl.BlockSpec(memory_space=pltpu.SMEM)
VMEM = pl.BlockSpec(memory_space=pltpu.VMEM)


def call(body, outs, inputs, name, scratch=(), specs=None, flops=0, moved=1 << 18):
    return pl.pallas_call(
        body,
        out_shape=outs,
        in_specs=specs or [VMEM] * len(inputs),
        out_specs=jax.tree.map(lambda _: VMEM, outs),
        scratch_shapes=scratch,
        compiler_params=pltpu.CompilerParams(vmem_limit_bytes=16 * 1024 * 1024),
        cost_estimate=pl.CostEstimate(flops=flops, bytes_accessed=moved, transcendentals=0),
        name=name,
    )(*inputs)


def plan_kernel(order, lengths, plan_ref, span_ref, *, group):
    zl, y, core = lax.axis_index("zl"), lax.axis_index("y"), lax.axis_index("core")
    ends, total = [], 0
    for k in range(lengths.shape[0]):
        total = total + lengths[k]
        ends.append(total)

    def put(row, value):
        plan_ref[row : row + 1, :] = jnp.full((1, LANES), value, jnp.int32)

    cols = span_ref.shape[1]
    for j in range(2):
        me = order[(zl * NY + y) * NCORE + (core ^ j)]
        q_first = me * BLK
        mine = jnp.maximum(lax.shift_right_logical(me, 1) - 2, 0)
        for m in range(4):
            near = order[(zl * NY + (y ^ m)) * NCORE + (core ^ j)]
            first = jnp.maximum(lax.shift_right_logical(near, 1) - 2, 0)
            pair = jnp.minimum(first + ((y - first) & 3), 15)
            want = lax.shift_right_logical(pair, 2)
            put(SEND + 2 * m + j, zl ^ want)
            put(WANT + 2 * m + j, want)
            offset = ((y ^ m) - mine) & 3
            low = ((mine + offset) * 2 + core) * BLK
            put(BASE + 2 * m + j, low)
        pos = q_first + lax.broadcasted_iota(jnp.int32, (1, cols), 1) // group
        start = jnp.zeros((1, cols), jnp.int32)
        for end in ends:
            start = jnp.where(end <= pos, end, start)
        span_ref[2 * j : 2 * j + 1, :] = start
        span_ref[2 * j + 1 : 2 * j + 2, :] = pos


def select_kernel(plan, own, col1, col2, col3, *outs):
    column = (own, col1, col2, col3)
    for m in range(4):
        for j in range(2):
            row = SEND + 2 * m + j
            at = jnp.concatenate([plan[row : row + 1, :]] * (own.shape[1] // LANES), axis=1)
            block = own[...]
            for s in range(1, 4):
                block = jnp.where(at == s, column[s][...], block)
            outs[m][j * BLK : (j + 1) * BLK, :] = block


def class_kernel(plan, q0, do0, stats0, q1, do1, stats1, span, kv, before, part_ref, ds_ref, after, *, m):
    rows, dh = q0.shape
    scale = dh ** (-0.5)
    after[...] = before[...]
    sides = ((q0, do0, stats0), (q1, do1, stats1))
    grads = [None, None]
    for c in range(rows // CHUNK):
        cols = slice(c * CHUNK, (c + 1) * CHUNK)
        for j, (q_ref, do_ref, stats) in enumerate(sides):
            keys = slice(j * BLK, (j + 1) * BLK)
            row = BASE + 2 * m + j
            key_pos = lax.broadcasted_iota(jnp.int32, (BLK, 1), 0) + plan[row : row + 1, 0:1]
            allowed = (key_pos >= span[2 * j : 2 * j + 1, cols]) & (key_pos <= span[2 * j + 1 : 2 * j + 2, cols])
            q = q_ref[cols, :]
            do = do_ref[cols, :]
            s = lax.dot_general(kv[keys, :dh], q, NT, preferred_element_type=jnp.float32)
            dp = lax.dot_general(kv[keys, dh:], do, NT, preferred_element_type=jnp.float32)
            p = jnp.where(allowed, jnp.exp2(s * (scale * LOG2E) - stats[0:1, cols]), 0.0)
            ds = (p * (dp - stats[1:2, cols])).astype(jnp.bfloat16)
            ds_ref[keys, cols] = ds
            dv = jnp.dot(p.astype(jnp.bfloat16), do, preferred_element_type=jnp.float32)
            dk = jnp.dot(ds, q, preferred_element_type=jnp.float32)
            grads[j] = (dk, dv) if c == 0 else (grads[j][0] + dk, grads[j][1] + dv)
    for j, (dk, dv) in enumerate(grads):
        keys = slice(j * BLK, (j + 1) * BLK)
        part_ref[keys, :dh] = (dk * scale).astype(part_ref.dtype)
        part_ref[keys, dh:] = dv.astype(part_ref.dtype)


def query_kernel(kv0, kv1, kv2, kv3, ds0, ds1, ds2, ds3, before, mine, theirs, after, kt):
    rows, dh = mine.shape
    after[...] = before[...]
    for j, out in enumerate((mine, theirs)):
        keys = slice(j * BLK, (j + 1) * BLK)
        for m, kv in enumerate((kv0, kv1, kv2, kv3)):
            kt[:, m * BLK : (m + 1) * BLK] = kv[keys, :dh].T

        def step(c, carry):
            cols = pl.ds(pl.multiple_of(c * CHUNK, CHUNK), CHUNK)
            ds = jnp.concatenate([ref[keys, cols] for ref in (ds0, ds1, ds2, ds3)], axis=0)
            dq = jnp.dot(kt[...], ds, preferred_element_type=jnp.float32)
            out[cols, :] = (dq * dh ** (-0.5)).T.astype(out.dtype)
            return carry

        lax.fori_loop(0, rows // CHUNK, step, 0)


def join_kernel(mine, theirs, out):
    out[...] = (mine[...] + theirs[...].astype(jnp.float32)).astype(out.dtype)


def total_kernel(plan, part0, part1, part2, part3, before, out, acc):
    acc[...] = jnp.zeros_like(acc)
    for m, part in enumerate((part0, part1, part2, part3)):
        for j in range(2):
            row = WANT + 2 * m + j
            z = jnp.max(plan[row : row + 1, :])
            acc[z] += part[j * BLK : (j + 1) * BLK, :].astype(jnp.float32)
    for z in range(ZL):
        for k in range(KVH):
            share = acc.shape[1] // KVH
            out[k % ZH * NX + k // ZH, z] = acc[z, k * share : (k + 1) * share, :].astype(out.dtype)


def finish_kernel(moved, gk_ref, gv_ref):
    dh = moved.shape[2] // 2
    for k in range(KVH):
        grad = moved[(k % ZH * NX + k // ZH) * ZL].astype(jnp.float32)
        for z in range(1, ZL):
            grad += moved[(k % ZH * NX + k // ZH) * ZL + z].astype(jnp.float32)
        gk_ref[:, k * dh : (k + 1) * dh] = grad[:, :dh].astype(gk_ref.dtype)
        gv_ref[:, k * dh : (k + 1) * dh] = grad[:, dh:].astype(gv_ref.dtype)


def swap(x, axis, size, mask):
    return lax.ppermute(x, axis, [(i, i ^ mask) for i in range(size)])


def local(queries, keys, values, outputs, out_grad, logsumexp, doc_lengths, block_order):
    rows, heads, dh = queries.shape
    cols = rows * heads
    wide = 2 * dh
    bf16, f32 = jnp.bfloat16, jnp.float32
    shape = jax.ShapeDtypeStruct

    own = jnp.concatenate([keys[:, 0, :], values[:, 0, :]], axis=1)
    column = [own] + [swap(own, "zl", ZL, m) for m in (1, 2, 3)]
    plan, span = call(
        functools.partial(plan_kernel, group=heads),
        (shape((24, LANES), jnp.int32), shape((4, cols), jnp.int32)),
        (block_order, doc_lengths), "plan", specs=[SMEM, SMEM],
    )
    delta = jnp.sum(out_grad.astype(f32) * outputs.astype(f32), axis=2)
    stats = jnp.stack([(logsumexp * LOG2E).T.reshape(-1), delta.reshape(-1)])
    sides = []
    for x in (queries.reshape(cols, dh), out_grad.reshape(cols, dh), stats):
        sides.append((x, swap(x, "core", NCORE, 1)))
    near, far = zip(*sides)

    pair = shape((2 * BLK, wide), bf16)
    sends = call(select_kernel, (pair,) * 4, (plan, *column), "select")
    kvs = [sends[0]] + [swap(sends[m], "y", NY, m) for m in (1, 2, 3)]
    token = jnp.zeros((8, LANES), f32)
    parts, dss = [None] * 4, [None] * 4
    for m in ORDER:
        parts[m], dss[m], token = call(
            functools.partial(class_kernel, m=m),
            (shape((2 * BLK, wide), f32 if m == 0 else bf16), shape((2 * BLK, cols), bf16), shape((8, LANES), f32)),
            (plan, *near, *far, span, kvs[m], token), "class" + str(m),
            flops=0, moved=1 << 12,
        )
    back = [parts[0]] + [swap(parts[m], "y", NY, m) for m in (1, 2, 3)]
    mine, theirs, token = call(
        query_kernel, (shape((cols, dh), f32), shape((cols, dh), bf16), shape((8, LANES), f32)),
        (*kvs, *dss, token), "query", scratch=[pltpu.VMEM((dh, 4 * BLK), bf16)],
        flops=0, moved=1<<12,
    )
    grad_q = call(join_kernel, shape((cols, dh), bf16), (mine, swap(theirs, "core", NCORE, 1)), "join", moved=1 << 21)

    total = call(
        total_kernel, shape((KVH, ZL, BLK // KVH, wide), bf16), (plan, *back, token), "total",
        scratch=[pltpu.VMEM((ZL, BLK, wide), f32)],
    )
    share = BLK // KVH
    moved = lax.all_to_all(
        total.reshape(ZL * KVH, share, wide), ("zh", "x", "zl"), split_axis=0, concat_axis=0, tiled=True
    )
    out = shape((share, KVH * dh), bf16)
    grad_keys, grad_values = call(finish_kernel, (out, out), (moved,), "finish")
    return grad_q.reshape(rows, heads, dh), grad_keys, grad_values


def solution(mesh):
    fine = Mesh(mesh.devices.reshape(ZL, NY, NCORE, NX, ZH), ("zl", "y", "core", "x", "zh"))
    ctx, kv = ("zl", "y", "core"), ("x", "zh")
    in_specs = (P(ctx, kv, None),) * 5 + (P(kv, ctx), P(), P())
    out_specs = (P(ctx, kv, None), P(ctx + kv, None), P(ctx + kv, None))
    return jax.shard_map(local, mesh=fine, in_specs=in_specs, out_specs=out_specs, check_vma=False)
```
